32 devices in a mesh: pts: 16 (over z, x, core), lab: 2 (over y).
Axes of the slice: x: 2, y: 2, z: 4, core: 2. Of those that a mesh axis runs over, the one named last changes fastest.
Arguments:
- slab_points: bfloat16 [1024, 128], P('pts'), may hold values from -6 to 6
- key_points: bfloat16 [16384, 128], P('pts'), may hold values from -6 to 6
- length_weights: float32 [128], replicated, may hold values from 0.5 to 2
- adjoint: bfloat16 [16384, 256], P('pts', 'lab'), may hold values from -2.5 to 2.5
- label_cov: float32 [256, 256], P('lab'), may hold values from -0.375 to 0.375
- cotangent: bfloat16 [1024, 256], P('pts', 'lab'), may hold values from -0.1875 to 0.1875
Outputs:
- mixed_rows: bfloat16 [1024, 256], P('pts', 'lab')
- cov_grad: float32 [256, 256], P('lab')
The draws below stay inside these ranges and needn't reach their ends.
All inputs are finite; a program needn't handle non-finite values.
Results may differ from the reference program's by a relative error of at most 0.005.
Values may be sent and summed in bfloat16 or wider, within the bound.
A program may use at most 64 MiB of HBM per device.

```python
import math
import jax
import jax.numpy as jnp
from jax import lax

F = 128
L = 256
KEY_DEV = 1024
NKEYS = 16384
SLAB = 1024


def block_levels(rng, dims, split, least, largest):
    loudness = 1.0
    for dim, parts in split:
        heights = jax.random.uniform(jax.random.fold_in(jax.random.fold_in(rng, 6), dim), (parts,), jnp.float32, least / len(split), largest / len(split))
        loudness = loudness * jnp.repeat(jnp.exp(heights), dims[dim] // parts).reshape((-1,) + (1,) * (len(dims) - 1 - dim))
    return loudness


def gaussian(own_key, dims, deviation, reach, cuts=(), kind=jnp.bfloat16):
    loudness = block_levels(own_key, dims, cuts, -0.22, 0.18) if cuts else 1.0
    result = jax.random.normal(own_key, dims, jnp.float32) * deviation * loudness
    return jnp.minimum(jnp.maximum(result, -reach), reach).astype(kind)


def setup_inputs(seed: int = 0) -> dict:
    streams_of = jax.random.split(jax.random.key(seed), 7)
    slab_points = gaussian(streams_of[0], (SLAB, F), 1.0, 6.0, ((0, 16),))
    key_points = gaussian(streams_of[1], (NKEYS, F), 1.0, 6.0, ((0, 16),))
    length_weights = jnp.clip(jnp.exp(jax.random.uniform(streams_of[2], (F,), jnp.float32, math.log(0.5), math.log(2.0))), 0.5, 2.0)
    adjoint = gaussian(streams_of[3], (NKEYS, L), (50.0 / NKEYS ** 0.5), 2.5, ((0, 16), (1, 2)))
    label_cov = gaussian(streams_of[4], (L, L), L ** -0.5, 0.375, ((0, 2),), jnp.float32)
    cotangent = gaussian(streams_of[5], (SLAB, L), (1.0 / SLAB ** 0.5), 0.1875, ((0, 16), (1, 2)))
    return {"slab_points": slab_points, "key_points": key_points, "length_weights": length_weights, "adjoint": adjoint, "label_cov": label_cov, "cotangent": cotangent}


def sq_norms(rows, weights):
    wide = rows.astype(jnp.float32)
    return jnp.sum(wide * wide * weights, axis=1)


def kernel_tile(slab_rows, slab_sq, scaled_keys, key_sq, width):
    inner = lax.dot_general(slab_rows, scaled_keys, (((1,), (1,)), ((), ())), preferred_element_type=jnp.float32)
    dist = slab_sq[:, None] + key_sq[None, :] - 2.0 * inner
    return jnp.exp(dist * (-2.0 / width)).astype(jnp.bfloat16)


def reference(slab_points, key_points, length_weights, adjoint, label_cov, cotangent):
    width = slab_points.shape[1]
    slab_sq = sq_norms(slab_points, length_weights)
    scaled = (key_points.astype(jnp.float32) * length_weights).astype(jnp.bfloat16)
    key_sq = sq_norms(key_points, length_weights)
    blocks = key_points.shape[0] // KEY_DEV

    def step(total, index):
        start = (index * KEY_DEV).astype(jnp.int32)
        keys_block = lax.dynamic_slice_in_dim(scaled, start, KEY_DEV, 0)
        sq_block = lax.dynamic_slice_in_dim(key_sq, start, KEY_DEV, 0)
        adj_block = lax.dynamic_slice_in_dim(adjoint, start, KEY_DEV, 0)
        tile = kernel_tile(slab_points, slab_sq, keys_block, sq_block, width)
        return total + jnp.dot(tile, adj_block, preferred_element_type=jnp.float32), None

    start_total = jnp.zeros((slab_points.shape[0], adjoint.shape[1]), jnp.float32)
    cross, _ = lax.scan(step, start_total, jnp.arange(blocks, dtype=jnp.int32))
    mixed = jnp.dot(cross, label_cov, precision=lax.Precision.HIGHEST, preferred_element_type=jnp.float32).astype(jnp.bfloat16)
    grad = jnp.dot(cross.T, cotangent.astype(jnp.float32), precision=lax.Precision.HIGHEST, preferred_element_type=jnp.float32)
    return mixed, grad
```

```python
import functools

import jax
import jax.numpy as jnp
from jax import lax
from jax.experimental import pallas as pl
from jax.experimental.pallas import tpu as pltpu
from jax.sharding import PartitionSpec as P

MESH = pl.DeviceIdType.MESH
HIGHEST = lax.Precision.HIGHEST
GROUP = 4
CHUNK = 16


def kernel(
    n, chunks,
    slab_hbm, key_hbm, w_hbm, adj_hbm, cov_hbm, cot_hbm,
    mixed_ref, grad_ref,
    key, w, adj, cov, cot, slab_all, part, got, mix_out, mix_in, gpart, ggot, gown, gall,
    scaled_t, key_term,
    loc, slab_send, slab_recv, part_send, part_recv, cot_send, cot_recv,
    mix_send, mix_recv, g_send, g_recv, f_send, f_recv,
):
    me = lax.axis_index("pts")
    lab = lax.axis_index("lab")
    other = 1 - lab
    groups = n // GROUP
    g_me = me // GROUP
    j_me = lax.rem(me, GROUP)
    rows, width = slab_hbm.shape
    half = adj_hbm.shape[1]
    strips = half // CHUNK

    def greet(k, c):
        pl.semaphore_signal(
            barrier, inc=1, device_id=(lax.rem(me + k, n), lab), device_id_type=MESH
        )
        return c

    barrier = pltpu.get_barrier_semaphore()
    lax.fori_loop(1, n, greet, 0)
    pl.semaphore_signal(barrier, inc=1, device_id=(me, other), device_id_type=MESH)

    loads = [
        pltpu.make_async_copy(src, dst, loc.at[i])
        for i, (src, dst) in enumerate(
            ((key_hbm, key), (w_hbm, w), (adj_hbm, adj), (cov_hbm, cov), (cot_hbm, cot.at[lab]))
        )
    ]
    for copy in loads:
        copy.start()
    pltpu.make_async_copy(slab_hbm, slab_all.at[me], slab_recv.at[g_me]).start()
    pl.semaphore_wait(barrier, n)

    def member(g, j):
        return g * GROUP + lax.rem(j_me + j, GROUP)

    def send_slab(q):
        pltpu.make_async_remote_copy(
            src_ref=slab_hbm, dst_ref=slab_all.at[me], send_sem=slab_send,
            recv_sem=slab_recv.at[g_me], device_id=(q, lab), device_id_type=MESH,
        ).start()

    for j in range(1, GROUP):
        send_slab(member(g_me, j))

    def send_group(k, c):
        g = lax.rem(g_me + groups - k, groups)
        for j in range(GROUP):
            send_slab(member(g, j))
        return c

    lax.fori_loop(1, groups, send_group, 0)
    cot_copy = pltpu.make_async_remote_copy(
        src_ref=cot_hbm, dst_ref=cot.at[lab], send_sem=cot_send, recv_sem=cot_recv,
        device_id=(me, other), device_id_type=MESH,
    )
    cot_copy.start()

    loads[0].wait()
    loads[1].wait()
    w_row = w[...]
    w_col = jnp.broadcast_to(w_row, (8, width)).T[:, :1]
    key_t = key[...].astype(jnp.float32).T
    weighted = key_t * w_col
    scaled_t[...] = weighted.astype(jnp.bfloat16)
    key_term[...] = jnp.sum(weighted * key_t, axis=0, keepdims=True) * (-2.0 / width)
    loads[2].wait()

    def partial(g):
        block = slab_all.at[pl.ds(g * GROUP, GROUP)]
        pltpu.make_async_copy(block, block, slab_recv.at[g]).wait()
        s = block[...].reshape(GROUP * rows, width)
        wide = s.astype(jnp.float32)
        s_term = jnp.sum(wide * wide * w_row, axis=1, keepdims=True) * (-2.0 / width)
        inner = jnp.dot(s, scaled_t[...], preferred_element_type=jnp.float32)
        tile = jnp.exp((s_term + key_term[...]) + inner * (4.0 / width)).astype(jnp.bfloat16)
        sums = jnp.dot(tile, adj[...], preferred_element_type=jnp.float32)
        part[pl.ds(g * GROUP, GROUP)] = sums.astype(jnp.bfloat16).reshape(GROUP, rows, half)

    def send_part(q):
        pltpu.make_async_remote_copy(
            src_ref=part.at[q], dst_ref=got.at[me], send_sem=part_send,
            recv_sem=part_recv, device_id=(q, lab), device_id_type=MESH,
        ).start()

    partial(g_me)
    pltpu.make_async_copy(part.at[me], got.at[me], part_recv).start()
    for j in range(1, GROUP):
        send_part(member(g_me, j))

    def step(k, c):
        g = lax.rem(g_me + k, groups)
        partial(g)
        for j in range(GROUP):
            send_part(member(g, j))
        return c

    lax.fori_loop(1, groups, step, 0)

    for copy in loads[3:]:
        copy.wait()
    cot_copy.wait()
    pltpu.make_async_copy(got, got, part_recv).wait()
    cross = jnp.sum(got[...].astype(jnp.float32), axis=0)

    cross_t = cross.T
    high = cross_t.astype(jnp.bfloat16)
    low = (cross_t - high.astype(jnp.float32)).astype(jnp.bfloat16)
    for h in range(2):
        c_half = cot[h]
        g_half = jnp.dot(high, c_half, preferred_element_type=jnp.float32) + jnp.dot(
            low, c_half, preferred_element_type=jnp.float32
        )
        gpart[h * strips:(h + 1) * strips] = g_half.astype(jnp.bfloat16).reshape(
            strips, CHUNK, half
        )

    def send_grad(q):
        pltpu.make_async_remote_copy(
            src_ref=gpart.at[q], dst_ref=ggot.at[me], send_sem=g_send,
            recv_sem=g_recv, device_id=(q, lab), device_id_type=MESH,
        ).start()

    def send_fin(q):
        pltpu.make_async_remote_copy(
            src_ref=gown, dst_ref=gall.at[me], send_sem=f_send,
            recv_sem=f_recv, device_id=(q, lab), device_id_type=MESH,
        ).start()

    def spread(k, c):
        send_grad(lax.rem(me + k, n))
        return c

    def spread_some(q, c):
        @pl.when(q != me)
        def _():
            send_grad(q)
        return c

    if n == chunks:
        lax.fori_loop(1, n, spread, 0)
    else:
        lax.fori_loop(0, chunks, spread_some, 0)

    def mixed_part(which):
        columns = pl.ds(pl.multiple_of(which * half, half), half)
        return jnp.dot(
            cross, cov[:, columns], precision=HIGHEST, preferred_element_type=jnp.float32
        )

    mix_out[...] = mixed_part(other)
    mix_copy = pltpu.make_async_remote_copy(
        src_ref=mix_out, dst_ref=mix_in, send_sem=mix_send, recv_sem=mix_recv,
        device_id=(me, other), device_id_type=MESH,
    )
    mix_copy.start()
    mixed_own = mixed_part(lab)

    def reduce_own():
        pltpu.make_async_copy(gpart.at[me], ggot.at[me], g_recv).start()
        pltpu.make_async_copy(ggot, ggot, g_recv).wait()
        gown[...] = jnp.sum(ggot[...].astype(jnp.float32), axis=0).astype(jnp.bfloat16)
        pltpu.make_async_copy(gown, gall.at[me], f_recv).start()

        def fan(k, c):
            send_fin(lax.rem(me + k, n))
            return c

        lax.fori_loop(1, n, fan, 0)

    if n == chunks:
        reduce_own()
    else:
        pl.when(me < chunks)(reduce_own)

    mix_copy.wait()
    mixed_ref[...] = (mixed_own + mix_in[...]).astype(jnp.bfloat16)

    pltpu.make_async_copy(gall, gall, f_recv).wait()
    for h in range(2):
        grad_ref[:, h * half:(h + 1) * half] = (
            gall[h * strips:(h + 1) * strips].reshape(half, half).astype(jnp.float32)
        )

    rest = slab_all.at[pl.ds(0, n - 1)]
    pltpu.make_async_copy(rest, rest, slab_send).wait()
    rest = part.at[pl.ds(0, n - 1)]
    pltpu.make_async_copy(rest, rest, part_send).wait()

    def drain_grad(count):
        piece = gpart.at[pl.ds(0, count)]
        pltpu.make_async_copy(piece, piece, g_send).wait()

    def drain_fin():
        sent = ggot.at[pl.ds(0, n - 1)]
        pltpu.make_async_copy(sent, sent, f_send).wait()

    if n == chunks:
        drain_grad(chunks - 1)
        drain_fin()
    else:
        @pl.when(me < chunks)
        def _():
            drain_grad(chunks - 1)
            drain_fin()

        @pl.when(me >= chunks)
        def _():
            drain_grad(chunks)


def local(n, slab_points, key_points, length_weights, adjoint, label_cov, cotangent):
    rows, width = slab_points.shape
    keys, half = adjoint.shape
    labels = label_cov.shape[1]
    chunks = (half // CHUNK) * (labels // half)
    bf16, f32 = jnp.bfloat16, jnp.float32
    dma = pltpu.SemaphoreType.DMA
    return pl.pallas_call(
        functools.partial(kernel, n, chunks),
        out_shape=(
            jax.ShapeDtypeStruct((rows, half), bf16),
            jax.ShapeDtypeStruct((half, labels), f32),
        ),
        in_specs=[pl.BlockSpec(memory_space=pl.ANY)] * 6,
        out_specs=[pl.BlockSpec(memory_space=pltpu.VMEM)] * 2,
        scratch_shapes=[
            pltpu.VMEM((keys, width), bf16),
            pltpu.VMEM((1, width), f32),
            pltpu.VMEM((keys, half), bf16),
            pltpu.VMEM((half, labels), f32),
            pltpu.VMEM((2, rows, half), bf16),
            pltpu.VMEM((n, rows, width), bf16),
            pltpu.VMEM((n, rows, half), bf16),
            pltpu.VMEM((n, rows, half), bf16),
            pltpu.VMEM((rows, half), f32),
            pltpu.VMEM((rows, half), f32),
            pltpu.VMEM((chunks, CHUNK, half), bf16),
            pltpu.VMEM((n, CHUNK, half), bf16),
            pltpu.VMEM((CHUNK, half), bf16),
            pltpu.VMEM((chunks, CHUNK, half), bf16),
            pltpu.VMEM((width, keys), bf16),
            pltpu.VMEM((1, keys), f32),
            dma((5,)),
            dma, dma((n // GROUP,)), dma, dma, dma, dma, dma, dma, dma, dma, dma, dma,
        ],
        compiler_params=pltpu.CompilerParams(
            collective_id=0, has_side_effects=True, vmem_limit_bytes=40 * 1024 * 1024
        ),
    )(slab_points, key_points, length_weights.reshape(1, width), adjoint, label_cov, cotangent)


def solution(mesh):
    placed = (P("pts", None), P("pts", None), P(), P("pts", "lab"), P("lab", None), P("pts", "lab"))
    return jax.shard_map(
        functools.partial(local, mesh.shape["pts"]),
        mesh=mesh,
        in_specs=placed,
        out_specs=(P("pts", "lab"), P("lab", None)),
        check_vma=False,
    )
```

```python
import functools

import jax
import jax.numpy as jnp
from jax import lax
from jax.experimental import pallas as pl
from jax.experimental.pallas import tpu as pltpu
from jax.sharding import PartitionSpec as P

MESH = pl.DeviceIdType.MESH
HIGHEST = lax.Precision.HIGHEST
GROUP = 4
CHUNK = 16


def kernel(
    n, chunks,
    slab_hbm, key_hbm, w_hbm, adj_hbm, cov_hbm, cot_hbm,
    mixed_ref, grad_ref,
    key, w, adj, cov, cot, slab_all, part, got, mix_out, mix_in, gpart, ggot, gown, gall,
    scaled_t, key_term,
    loc, slab_send, slab_recv, part_send, part_recv, cot_send, cot_recv,
    mix_send, mix_recv, g_send, g_recv, f_send, f_recv,
):
    me = lax.axis_index("pts")
    lab = lax.axis_index("lab")
    other = 1 - lab
    groups = n // GROUP
    g_me = me // GROUP
    j_me = lax.rem(me, GROUP)
    rows, width = slab_hbm.shape
    half = adj_hbm.shape[1]
    strips = half // CHUNK

    def greet(k, c):
        pl.semaphore_signal(
            barrier, inc=1, device_id=(lax.rem(me + k, n), lab), device_id_type=MESH
        )
        return c

    barrier = pltpu.get_barrier_semaphore()
    lax.fori_loop(1, n, greet, 0)
    pl.semaphore_signal(barrier, inc=1, device_id=(me, other), device_id_type=MESH)

    loads = [
        pltpu.make_async_copy(src, dst, loc.at[i])
        for i, (src, dst) in enumerate(
            ((key_hbm, key), (w_hbm, w), (adj_hbm, adj), (cov_hbm, cov), (cot_hbm, cot.at[lab]))
        )
    ]
    for copy in loads:
        copy.start()
    pltpu.make_async_copy(slab_hbm, slab_all.at[me], slab_recv.at[g_me]).start()
    pl.semaphore_wait(barrier, n)

    def member(g, j):
        return g * GROUP + lax.rem(j_me + j, GROUP)

    def send_slab(q):
        pltpu.make_async_remote_copy(
            src_ref=slab_hbm, dst_ref=slab_all.at[me], send_sem=slab_send,
            recv_sem=slab_recv.at[g_me], device_id=(q, lab), device_id_type=MESH,
        ).start()

    for j in range(1, GROUP):
        send_slab(member(g_me, j))

    def send_group(k, c):
        g = lax.rem(g_me + groups - k, groups)
        for j in range(GROUP):
            send_slab(member(g, j))
        return c

    lax.fori_loop(1, groups, send_group, 0)
    cot_copy = pltpu.make_async_remote_copy(
        src_ref=cot_hbm, dst_ref=cot.at[lab], send_sem=cot_send, recv_sem=cot_recv,
        device_id=(me, other), device_id_type=MESH,
    )
    cot_copy.start()

    loads[0].wait()
    loads[1].wait()
    w_row = w[...]
    w_col = jnp.broadcast_to(w_row, (8, width)).T[:, :1]
    key_t = key[...].astype(jnp.float32).T
    weighted = key_t * w_col
    scaled_t[...] = weighted.astype(jnp.bfloat16)
    key_term[...] = jnp.sum(weighted * key_t, axis=0, keepdims=True) * (-2.0 / width)
    loads[2].wait()

    def partial(g):
        block = slab_all.at[pl.ds(g * GROUP, GROUP)]
        pltpu.make_async_copy(block, block, slab_recv.at[g]).wait()
        s = block[...].reshape(GROUP * rows, width)
        wide = s.astype(jnp.float32)
        s_term = jnp.sum(wide * wide * w_row, axis=1, keepdims=True) * (-2.0 / width)
        inner = jnp.dot(s, scaled_t[...], preferred_element_type=jnp.float32)
        tile = jnp.exp((s_term + key_term[...]) + inner * (4.0 / width)).astype(jnp.bfloat16)
        sums = jnp.dot(tile, adj[...], preferred_element_type=jnp.float32)
        part[pl.ds(g * GROUP, GROUP)] = sums.astype(jnp.bfloat16).reshape(GROUP, rows, half)

    def send_part(q):
        pltpu.make_async_remote_copy(
            src_ref=part.at[q], dst_ref=got.at[me], send_sem=part_send,
            recv_sem=part_recv, device_id=(q, lab), device_id_type=MESH,
        ).start()

    partial(g_me)
    pltpu.make_async_copy(part.at[me], got.at[me], part_recv).start()
    for j in range(1, GROUP):
        send_part(member(g_me, j))

    def step(k, c):
        g = lax.rem(g_me + k, groups)
        partial(g)
        for j in range(GROUP):
            send_part(member(g, j))
        return c

    lax.fori_loop(1, groups, step, 0)

    for copy in loads[3:]:
        copy.wait()
    cot_copy.wait()
    pltpu.make_async_copy(got, got, part_recv).wait()
    cross = jnp.sum(got[...].astype(jnp.float32), axis=0)

    cross_t = cross.T
    high = cross_t.astype(jnp.bfloat16)
    low = (cross_t - high.astype(jnp.float32)).astype(jnp.bfloat16)
    for h in range(2):
        c_half = cot[h]
        g_half = jnp.dot(high, c_half, preferred_element_type=jnp.float32) + jnp.dot(
            low, c_half, preferred_element_type=jnp.float32
        )
        gpart[h * strips:(h + 1) * strips] = g_half.astype(jnp.bfloat16).reshape(
            strips, CHUNK, half
        )

    def send_grad(q):
        pltpu.make_async_remote_copy(
            src_ref=gpart.at[q], dst_ref=ggot.at[me], send_sem=g_send,
            recv_sem=g_recv, device_id=(q, lab), device_id_type=MESH,
        ).start()

    def send_fin(q):
        pltpu.make_async_remote_copy(
            src_ref=gown, dst_ref=gall.at[me], send_sem=f_send,
            recv_sem=f_recv, device_id=(q, lab), device_id_type=MESH,
        ).start()

    def spread(k, c):
        send_grad(lax.rem(me + k, n))
        return c

    def spread_some(q, c):
        @pl.when(q != me)
        def _():
            send_grad(q)
        return c

    if n == chunks:
        lax.fori_loop(1, n, spread, 0)
    else:
        lax.fori_loop(0, chunks, spread_some, 0)

    def mixed_part(which):
        columns = pl.ds(pl.multiple_of(which * half, half), half)
        return jnp.dot(
            cross, cov[:, columns], precision=HIGHEST, preferred_element_type=jnp.float32
        )

    mix_out[...] = mixed_part(other)
    mix_copy = pltpu.make_async_remote_copy(
        src_ref=mix_out, dst_ref=mix_in, send_sem=mix_send, recv_sem=mix_recv,
        device_id=(me, other), device_id_type=MESH,
    )
    mix_copy.start()
    mixed_own = mixed_part(lab)

    def reduce_own():
        pltpu.make_async_copy(gpart.at[me], ggot.at[me], g_recv).start()
        pltpu.make_async_copy(ggot, ggot, g_recv).wait()
        gown[...] = jnp.sum(ggot[...].astype(jnp.float32), axis=0).astype(jnp.bfloat16)
        pltpu.make_async_copy(gown, gall.at[me], f_recv).start()

        def fan(k, c):
            send_fin(lax.rem(me + k, n))
            return c

        lax.fori_loop(1, n, fan, 0)

    if n == chunks:
        reduce_own()
    else:
        pl.when(me < chunks)(reduce_own)

    mix_copy.wait()
    mixed_ref[...] = (mixed_own + mix_in[...]).astype(jnp.bfloat16)

    pltpu.make_async_copy(gall, gall, f_recv).wait()
    for h in range(2):
        grad_ref[:, h * half:(h + 1) * half] = (
            gall[h * strips:(h + 1) * strips].reshape(half, half).astype(jnp.float32)
        )

    rest = slab_all.at[pl.ds(0, n - 1)]
    pltpu.make_async_copy(rest, rest, slab_send).wait()
    rest = part.at[pl.ds(0, n - 1)]
    pltpu.make_async_copy(rest, rest, part_send).wait()

    def drain_grad(count):
        piece = gpart.at[pl.ds(0, count)]
        pltpu.make_async_copy(piece, piece, g_send).wait()

    def drain_fin():
        sent = ggot.at[pl.ds(0, n - 1)]
        pltpu.make_async_copy(sent, sent, f_send).wait()

    if n == chunks:
        drain_grad(chunks - 1)
        drain_fin()
    else:
        @pl.when(me < chunks)
        def _():
            drain_grad(chunks - 1)
            drain_fin()

        @pl.when(me >= chunks)
        def _():
            drain_grad(chunks)


def local(n, slab_points, key_points, length_weights, adjoint, label_cov, cotangent):
    rows, width = slab_points.shape
    keys, half = adjoint.shape
    labels = label_cov.shape[1]
    chunks = (half // CHUNK) * (labels // half)
    bf16, f32 = jnp.bfloat16, jnp.float32
    dma = pltpu.SemaphoreType.DMA
    return pl.pallas_call(
        functools.partial(kernel, n, chunks),
        out_shape=(
            jax.ShapeDtypeStruct((rows, half), bf16),
            jax.ShapeDtypeStruct((half, labels), f32),
        ),
        in_specs=[pl.BlockSpec(memory_space=pltpu.HBM)] * 6,
        out_specs=[pl.BlockSpec(memory_space=pltpu.VMEM)] * 2,
        scratch_shapes=[
            pltpu.VMEM((keys, width), bf16),
            pltpu.VMEM((1, width), f32),
            pltpu.VMEM((keys, half), bf16),
            pltpu.VMEM((half, labels), f32),
            pltpu.VMEM((2, rows, half), bf16),
            pltpu.VMEM((n, rows, width), bf16),
            pltpu.VMEM((n, rows, half), bf16),
            pltpu.VMEM((n, rows, half), bf16),
            pltpu.VMEM((rows, half), f32),
            pltpu.VMEM((rows, half), f32),
            pltpu.VMEM((chunks, CHUNK, half), bf16),
            pltpu.VMEM((n, CHUNK, half), bf16),
            pltpu.VMEM((CHUNK, half), bf16),
            pltpu.VMEM((chunks, CHUNK, half), bf16),
            pltpu.VMEM((width, keys), bf16),
            pltpu.VMEM((1, keys), f32),
            dma((5,)),
            dma, dma((n // GROUP,)), dma, dma, dma, dma, dma, dma, dma, dma, dma, dma,
        ],
        compiler_params=pltpu.CompilerParams(
            collective_id=0, has_side_effects=True, vmem_limit_bytes=60 * 1024 * 1024
        ),
    )(slab_points, key_points, length_weights.reshape(1, width), adjoint, label_cov, cotangent)


def solution(mesh):
    placed = (P("pts", None), P("pts", None), P(), P("pts", "lab"), P("lab", None), P("pts", "lab"))
    return jax.shard_map(
        functools.partial(local, mesh.shape["pts"]),
        mesh=mesh,
        in_specs=placed,
        out_specs=(P("pts", "lab"), P("lab", None)),
        check_vma=False,
    )
```

```python
import functools

import jax
import jax.numpy as jnp
from jax import lax
from jax.experimental import pallas as pl
from jax.experimental.pallas import tpu as pltpu
from jax.sharding import PartitionSpec as P

MESH = pl.DeviceIdType.MESH
HIGHEST = lax.Precision.HIGHEST
PAIR = 2
CHUNK = 16


def kernel(
    n, chunks,
    slab_hbm, key_hbm, w_hbm, adj_hbm, cov_hbm, cot_hbm,
    mixed_ref, grad_ref,
    key, w, adj, cov, cot, slab_all, pair_out, pair_in, kept, part, got, mix_out, mix_in, gpart, ggot, gown, gall,
    scaled_t, key_term,
    loc, slab_send, slab_recv, fwd_send, fwd_recv, pair_send, pair_recv, part_send, part_recv, cot_send, cot_recv,
    mix_send, mix_recv, g_send, g_recv, f_send, f_recv,
):
    me = lax.axis_index("pts")
    lab = lax.axis_index("lab")
    other = 1 - lab
    chip = me // 2
    core = lax.rem(me, 2)
    sibling = chip * 2 + 1 - core
    chips = n // 2
    groups = chips // PAIR
    unrolled = groups <= 4
    g_me = chip // PAIR
    rows, width = slab_hbm.shape
    half = adj_hbm.shape[1]
    strips = half // CHUNK

    def greet(k, c):
        pl.semaphore_signal(
            barrier, inc=1, device_id=(lax.rem(me + k, n), lab), device_id_type=MESH
        )
        return c

    barrier = pltpu.get_barrier_semaphore()
    lax.fori_loop(1, n, greet, 0)
    pl.semaphore_signal(barrier, inc=1, device_id=(me, other), device_id_type=MESH)

    loads = [
        pltpu.make_async_copy(src, dst, loc.at[i])
        for i, (src, dst) in enumerate(
            ((key_hbm, key), (w_hbm, w), (adj_hbm, adj), (cov_hbm, cov), (cot_hbm, cot.at[lab]))
        )
    ]
    for copy in loads:
        copy.start()
    mine = slab_all.at[core, chip]
    pltpu.make_async_copy(slab_hbm, mine, slab_recv.at[g_me]).start()
    pl.semaphore_wait(barrier, n)

    def send_slab(q):
        pltpu.make_async_remote_copy(
            src_ref=slab_hbm, dst_ref=mine, send_sem=slab_send,
            recv_sem=slab_recv.at[g_me], device_id=(q, lab), device_id_type=MESH,
        ).start()

    def member(g, j):
        return (g * PAIR + lax.rem(chip + j, PAIR)) * 2 + core

    send_slab(member(g_me, 1))
    for k in range(1, groups) if unrolled else ():
        for j in range(PAIR):
            send_slab(member(lax.rem(g_me + groups - k, groups), j))

    def send_group(k, c):
        for j in range(PAIR):
            send_slab(member(lax.rem(g_me + groups - k, groups), j))
        return c

    if not unrolled:
        lax.fori_loop(1, groups, send_group, 0)
    cot_copy = pltpu.make_async_remote_copy(
        src_ref=cot_hbm, dst_ref=cot.at[lab], send_sem=cot_send, recv_sem=cot_recv,
        device_id=(me, other), device_id_type=MESH,
    )
    cot_copy.start()

    loads[0].wait()
    loads[1].wait()
    w_row = w[...]
    w_col = jnp.broadcast_to(w_row, (8, width)).T[:, :1]
    key_t = key[...].astype(jnp.float32).T
    weighted = key_t * w_col
    scaled_t[...] = weighted.astype(jnp.bfloat16)
    key_term[...] = jnp.sum(weighted * key_t, axis=0, keepdims=True) * (-2.0 / width)

    def forward(g):
        block = slab_all.at[core, pl.ds(g * PAIR, PAIR)]
        pltpu.make_async_copy(block, block, slab_recv.at[g]).wait()
        pltpu.make_async_remote_copy(
            src_ref=block, dst_ref=block, send_sem=fwd_send, recv_sem=fwd_recv.at[g],
            device_id=(sibling, lab), device_id_type=MESH,
        ).start()

    def partial(g):
        block = slab_all.at[1 - core, pl.ds(g * PAIR, PAIR)]
        pltpu.make_async_copy(block, block, fwd_recv.at[g]).wait()
        own = slab_all[core, pl.ds(g * PAIR, PAIR)].reshape(PAIR * rows, width)
        s = jnp.concatenate([own, block[...].reshape(PAIR * rows, width)], axis=0)
        wide = s.astype(jnp.float32)
        s_term = jnp.sum(wide * wide * w_row, axis=1, keepdims=True) * (-2.0 / width)
        inner = jnp.dot(s, scaled_t[...], preferred_element_type=jnp.float32)
        tile = jnp.exp((s_term + key_term[...]) + inner * (4.0 / width)).astype(jnp.bfloat16)
        sums = jnp.dot(tile, adj[...], preferred_element_type=jnp.float32)
        pair_out[g] = sums[PAIR * rows:]
        pltpu.make_async_remote_copy(
            src_ref=pair_out.at[g], dst_ref=pair_in.at[g], send_sem=pair_send,
            recv_sem=pair_recv.at[g], device_id=(sibling, lab), device_id_type=MESH,
        ).start()
        kept[g] = sums[:PAIR * rows]

    def send_part(g, j):
        q = member(g, j)
        pltpu.make_async_remote_copy(
            src_ref=part.at[q // 2], dst_ref=got.at[chip], send_sem=part_send,
            recv_sem=part_recv, device_id=(q, lab), device_id_type=MESH,
        ).start()

    def collect(g):
        arrived = pair_in.at[g]
        pltpu.make_async_copy(arrived, arrived, pair_recv.at[g]).wait()
        both = (kept[g] + arrived[...]).astype(jnp.bfloat16)
        part[pl.ds(g * PAIR, PAIR)] = both.reshape(PAIR, rows, half)

    def group_at(k):
        return lax.rem(g_me + k, groups)

    forward(g_me)
    loads[2].wait()
    forward(group_at(1))
    partial(g_me)

    def step(k, c):
        @pl.when(k + 1 < groups)
        def _():
            forward(group_at(k + 1))
        partial(group_at(k))

        @pl.when(k == 1)
        def _():
            collect(g_me)
            pltpu.make_async_copy(part.at[chip], got.at[chip], part_recv).start()
            send_part(g_me, 1)

        @pl.when(k > 1)
        def _():
            g = group_at(k - 1)
            collect(g)
            for j in range(PAIR):
                send_part(g, j)
        return c

    if unrolled:
        for k in range(1, groups):
            if k + 1 < groups:
                forward(group_at(k + 1))
            partial(group_at(k))
            g = group_at(k - 1)
            collect(g)
            if k == 1:
                pltpu.make_async_copy(part.at[chip], got.at[chip], part_recv).start()
                send_part(g, 1)
            else:
                for j in range(PAIR):
                    send_part(g, j)
    else:
        lax.fori_loop(1, groups, step, 0)
    g = group_at(groups - 1)
    collect(g)
    for j in range(PAIR):
        send_part(g, j)

    for copy in loads[3:]:
        copy.wait()
    cot_copy.wait()
    pltpu.make_async_copy(got, got, part_recv).wait()
    cross = jnp.sum(got[...].astype(jnp.float32), axis=0)

    cross_t = cross.T
    high = cross_t.astype(jnp.bfloat16)
    low = (cross_t - high.astype(jnp.float32)).astype(jnp.bfloat16)
    for h in range(2):
        c_half = cot[h]
        g_half = jnp.dot(high, c_half, preferred_element_type=jnp.float32) + jnp.dot(
            low, c_half, preferred_element_type=jnp.float32
        )
        gpart[h * strips:(h + 1) * strips] = g_half.astype(jnp.bfloat16).reshape(
            strips, CHUNK, half
        )

    def send_grad(q):
        pltpu.make_async_remote_copy(
            src_ref=gpart.at[q], dst_ref=ggot.at[me], send_sem=g_send,
            recv_sem=g_recv, device_id=(q, lab), device_id_type=MESH,
        ).start()

    def send_fin(q):
        pltpu.make_async_remote_copy(
            src_ref=gown, dst_ref=gall.at[me], send_sem=f_send,
            recv_sem=f_recv, device_id=(q, lab), device_id_type=MESH,
        ).start()

    def spread(k, c):
        send_grad(lax.rem(me + k, n))
        return c

    def spread_some(q, c):
        @pl.when(q != me)
        def _():
            send_grad(q)
        return c

    if n == chunks:
        lax.fori_loop(1, n, spread, 0)
    else:
        lax.fori_loop(0, chunks, spread_some, 0)

    def mixed_part(which):
        columns = pl.ds(pl.multiple_of(which * half, half), half)
        return jnp.dot(
            cross, cov[:, columns], precision=HIGHEST, preferred_element_type=jnp.float32
        )

    mix_out[...] = mixed_part(other)
    mix_copy = pltpu.make_async_remote_copy(
        src_ref=mix_out, dst_ref=mix_in, send_sem=mix_send, recv_sem=mix_recv,
        device_id=(me, other), device_id_type=MESH,
    )
    mix_copy.start()
    mixed_own = mixed_part(lab)

    def reduce_own():
        pltpu.make_async_copy(gpart.at[me], ggot.at[me], g_recv).start()
        pltpu.make_async_copy(ggot, ggot, g_recv).wait()
        gown[...] = jnp.sum(ggot[...].astype(jnp.float32), axis=0).astype(jnp.bfloat16)
        pltpu.make_async_copy(gown, gall.at[me], f_recv).start()

        def fan(k, c):
            send_fin(lax.rem(me + k, n))
            return c

        lax.fori_loop(1, n, fan, 0)

    if n == chunks:
        reduce_own()
    else:
        pl.when(me < chunks)(reduce_own)

    mix_copy.wait()
    mixed_ref[...] = (mixed_own + mix_in[...]).astype(jnp.bfloat16)

    pltpu.make_async_copy(gall, gall, f_recv).wait()
    for h in range(2):
        grad_ref[:, h * half:(h + 1) * half] = (
            gall[h * strips:(h + 1) * strips].reshape(half, half).astype(jnp.float32)
        )

    rest = slab_all.at[0, pl.ds(0, chips - 1)]
    pltpu.make_async_copy(rest, rest, slab_send).wait()
    rest = part.at[pl.ds(0, chips - 1)]
    pltpu.make_async_copy(rest, rest, part_send).wait()
    pltpu.make_async_copy(slab_all.at[0], slab_all.at[0], fwd_send).wait()
    pltpu.make_async_copy(pair_out, pair_out, pair_send).wait()

    def drain_grad(count):
        piece = gpart.at[pl.ds(0, count)]
        pltpu.make_async_copy(piece, piece, g_send).wait()

    def drain_fin():
        sent = ggot.at[pl.ds(0, n - 1)]
        pltpu.make_async_copy(sent, sent, f_send).wait()

    if n == chunks:
        drain_grad(chunks - 1)
        drain_fin()
    else:
        @pl.when(me < chunks)
        def _():
            drain_grad(chunks - 1)
            drain_fin()

        @pl.when(me >= chunks)
        def _():
            drain_grad(chunks)


def local(n, slab_points, key_points, length_weights, adjoint, label_cov, cotangent):
    rows, width = slab_points.shape
    keys, half = adjoint.shape
    labels = label_cov.shape[1]
    chunks = (half // CHUNK) * (labels // half)
    bf16, f32 = jnp.bfloat16, jnp.float32
    dma = pltpu.SemaphoreType.DMA
    chips = n // 2
    groups = chips // PAIR
    return pl.pallas_call(
        functools.partial(kernel, n, chunks),
        out_shape=(
            jax.ShapeDtypeStruct((rows, half), bf16),
            jax.ShapeDtypeStruct((half, labels), f32),
        ),
        in_specs=[pl.BlockSpec(memory_space=pltpu.HBM)] * 6,
        out_specs=[pl.BlockSpec(memory_space=pltpu.VMEM)] * 2,
        scratch_shapes=[
            pltpu.VMEM((keys, width), bf16),
            pltpu.VMEM((1, width), f32),
            pltpu.VMEM((keys, half), bf16),
            pltpu.VMEM((half, labels), f32),
            pltpu.VMEM((2, rows, half), bf16),
            pltpu.VMEM((2, chips, rows, width), bf16),
            pltpu.VMEM((groups, PAIR * rows, half), f32),
            pltpu.VMEM((groups, PAIR * rows, half), f32),
            pltpu.VMEM((groups, PAIR * rows, half), f32),
            pltpu.VMEM((chips, rows, half), bf16),
            pltpu.VMEM((chips, rows, half), bf16),
            pltpu.VMEM((rows, half), f32),
            pltpu.VMEM((rows, half), f32),
            pltpu.VMEM((chunks, CHUNK, half), bf16),
            pltpu.VMEM((n, CHUNK, half), bf16),
            pltpu.VMEM((CHUNK, half), bf16),
            pltpu.VMEM((chunks, CHUNK, half), bf16),
            pltpu.VMEM((width, keys), bf16),
            pltpu.VMEM((1, keys), f32),
            dma((5,)),
            dma, dma((groups,)), dma, dma((groups,)), dma, dma((groups,)), dma, dma, dma, dma, dma, dma, dma, dma, dma, dma,
        ],
        compiler_params=pltpu.CompilerParams(
            collective_id=0, has_side_effects=True, vmem_limit_bytes=60 * 1024 * 1024
        ),
    )(slab_points, key_points, length_weights.reshape(1, width), adjoint, label_cov, cotangent)


def solution(mesh):
    placed = (P("pts", None), P("pts", None), P(), P("pts", "lab"), P("lab", None), P("pts", "lab"))
    return jax.shard_map(
        functools.partial(local, mesh.shape["pts"]),
        mesh=mesh,
        in_specs=placed,
        out_specs=(P("pts", "lab"), P("lab", None)),
        check_vma=False,
    )
```

```python
import functools

import jax
import jax.numpy as jnp
from jax import lax
from jax.experimental import pallas as pl
from jax.experimental.pallas import tpu as pltpu
from jax.sharding import PartitionSpec as P

MESH = pl.DeviceIdType.MESH
HIGHEST = lax.Precision.HIGHEST
PAIR = 2
CHUNK = 16


def kernel(
    n, chunks,
    slab_hbm, key_hbm, w_hbm, adj_hbm, cov_hbm, cot_hbm,
    mixed_ref, grad_ref,
    key, w, adj, cov, cot, slab_all, pair_out, pair_in, kept, part, got, mix_out, mix_in, gpart, ggot, gown, gall,
    scaled_t, key_term,
    loc, slab_send, slab_recv, fwd_send, fwd_recv, pair_send, pair_recv, part_send, part_recv, cot_send, cot_recv,
    mix_send, mix_recv, g_send, g_recv, f_send, f_recv,
):
    me = lax.axis_index("pts")
    lab = lax.axis_index("lab")
    other = 1 - lab
    chip = me // 2
    core = lax.rem(me, 2)
    sibling = chip * 2 + 1 - core
    chips = n // 2
    groups = chips // PAIR
    unrolled = groups <= 4
    g_me = chip // PAIR
    rows, width = slab_hbm.shape
    half = adj_hbm.shape[1]
    strips = half // CHUNK

    def greet(k, c):
        pl.semaphore_signal(
            barrier, inc=1, device_id=(lax.rem(me + k, n), lab), device_id_type=MESH
        )
        return c

    barrier = pltpu.get_barrier_semaphore()
    lax.fori_loop(1, n, greet, 0)
    pl.semaphore_signal(barrier, inc=1, device_id=(me, other), device_id_type=MESH)

    loads = [
        pltpu.make_async_copy(src, dst, loc.at[i])
        for i, (src, dst) in enumerate(
            ((key_hbm, key), (w_hbm, w), (adj_hbm, adj), (cov_hbm, cov), (cot_hbm, cot.at[lab]))
        )
    ]
    for copy in loads:
        copy.start()
    mine = slab_all.at[core, chip]
    pltpu.make_async_copy(slab_hbm, mine, slab_recv.at[g_me]).start()
    pl.semaphore_wait(barrier, n)

    def send_slab(q):
        pltpu.make_async_remote_copy(
            src_ref=slab_hbm, dst_ref=mine, send_sem=slab_send,
            recv_sem=slab_recv.at[g_me], device_id=(q, lab), device_id_type=MESH,
        ).start()

    def member(g, j):
        return (g * PAIR + lax.rem(chip + j, PAIR)) * 2 + core

    send_slab(member(g_me, 1))
    for k in range(1, groups) if unrolled else ():
        for j in range(PAIR):
            send_slab(member(lax.rem(g_me + groups - k, groups), j))

    def send_group(k, c):
        for j in range(PAIR):
            send_slab(member(lax.rem(g_me + groups - k, groups), j))
        return c

    if not unrolled:
        lax.fori_loop(1, groups, send_group, 0)
    cot_copy = pltpu.make_async_remote_copy(
        src_ref=cot_hbm, dst_ref=cot.at[lab], send_sem=cot_send, recv_sem=cot_recv,
        device_id=(me, other), device_id_type=MESH,
    )
    cot_copy.start()

    loads[0].wait()
    loads[1].wait()
    w_row = w[...]
    w_col = jnp.broadcast_to(w_row, (8, width)).T[:, :1]
    key_t = key[...].astype(jnp.float32).T
    weighted = key_t * w_col
    scaled_t[...] = weighted.astype(jnp.bfloat16)
    key_term[...] = jnp.sum(weighted * key_t, axis=0, keepdims=True) * (-2.0 / width)

    def forward(g):
        block = slab_all.at[core, pl.ds(g * PAIR, PAIR)]
        pltpu.make_async_copy(block, block, slab_recv.at[g]).wait()
        pltpu.make_async_remote_copy(
            src_ref=block, dst_ref=block, send_sem=fwd_send, recv_sem=fwd_recv.at[g],
            device_id=(sibling, lab), device_id_type=MESH,
        ).start()

    def partial(g):
        block = slab_all.at[1 - core, pl.ds(g * PAIR, PAIR)]
        pltpu.make_async_copy(block, block, fwd_recv.at[g]).wait()
        own = slab_all[core, pl.ds(g * PAIR, PAIR)].reshape(PAIR * rows, width)
        s = jnp.concatenate([own, block[...].reshape(PAIR * rows, width)], axis=0)
        wide = s.astype(jnp.float32)
        s_term = jnp.sum(wide * wide * w_row, axis=1, keepdims=True) * (-2.0 / width)
        inner = jnp.dot(s, scaled_t[...], preferred_element_type=jnp.float32)
        tile = jnp.exp((s_term + key_term[...]) + inner * (4.0 / width)).astype(jnp.bfloat16)
        sums = jnp.dot(tile, adj[...], preferred_element_type=jnp.float32)
        pair_out[g] = sums[PAIR * rows:]
        pltpu.make_async_remote_copy(
            src_ref=pair_out.at[g], dst_ref=pair_in.at[g], send_sem=pair_send,
            recv_sem=pair_recv.at[g], device_id=(sibling, lab), device_id_type=MESH,
        ).start()
        kept[g] = sums[:PAIR * rows]

    def send_part(g, j):
        q = member(g, j)
        pltpu.make_async_remote_copy(
            src_ref=part.at[q // 2], dst_ref=got.at[chip], send_sem=part_send,
            recv_sem=part_recv, device_id=(q, lab), device_id_type=MESH,
        ).start()

    def collect(g):
        arrived = pair_in.at[g]
        pltpu.make_async_copy(arrived, arrived, pair_recv.at[g]).wait()
        both = (kept[g] + arrived[...]).astype(jnp.bfloat16)
        part[pl.ds(g * PAIR, PAIR)] = both.reshape(PAIR, rows, half)

    def group_at(k):
        return lax.rem(g_me + k, groups)

    forward(g_me)
    loads[2].wait()
    forward(group_at(1))
    partial(g_me)

    def step(k, c):
        @pl.when(k + 1 < groups)
        def _():
            forward(group_at(k + 1))
        partial(group_at(k))

        @pl.when(k == 1)
        def _():
            collect(g_me)
            pltpu.make_async_copy(part.at[chip], got.at[chip], part_recv).start()
            send_part(g_me, 1)

        @pl.when(k > 1)
        def _():
            g = group_at(k - 1)
            collect(g)
            for j in range(PAIR):
                send_part(g, j)
        return c

    if unrolled:
        for k in range(1, groups):
            if k + 1 < groups:
                forward(group_at(k + 1))
            partial(group_at(k))
            g = group_at(k - 1)
            collect(g)
            if k == 1:
                pltpu.make_async_copy(part.at[chip], got.at[chip], part_recv).start()
                send_part(g, 1)
            else:
                for j in range(PAIR):
                    send_part(g, j)
    else:
        lax.fori_loop(1, groups, step, 0)
    g = group_at(groups - 1)
    collect(g)
    for j in range(PAIR):
        send_part(g, j)

    for copy in loads[3:]:
        copy.wait()
    cot_copy.wait()
    pltpu.make_async_copy(got, got, part_recv).wait()
    cross = jnp.sum(got[...].astype(jnp.float32), axis=0)

    cross_t = cross.T
    high = cross_t.astype(jnp.bfloat16)
    low = (cross_t - high.astype(jnp.float32)).astype(jnp.bfloat16)
    for h in range(2):
        c_half = cot[h]
        g_half = jnp.dot(high, c_half, preferred_element_type=jnp.float32) + jnp.dot(
            low, c_half, preferred_element_type=jnp.float32
        )
        gpart[h * strips:(h + 1) * strips] = g_half.astype(jnp.bfloat16).reshape(
            strips, CHUNK, half
        )

    def send_grad(q):
        pltpu.make_async_remote_copy(
            src_ref=gpart.at[q], dst_ref=ggot.at[me], send_sem=g_send,
            recv_sem=g_recv, device_id=(q, lab), device_id_type=MESH,
        ).start()

    def send_fin(q):
        pltpu.make_async_remote_copy(
            src_ref=gown, dst_ref=gall.at[me], send_sem=f_send,
            recv_sem=f_recv, device_id=(q, lab), device_id_type=MESH,
        ).start()

    def spread(k, c):
        send_grad(lax.rem(me + k, n))
        return c

    def spread_some(q, c):
        @pl.when(q != me)
        def _():
            send_grad(q)
        return c

    if n == chunks:
        lax.fori_loop(1, n, spread, 0)
    else:
        lax.fori_loop(0, chunks, spread_some, 0)

    def mixed_part(which):
        columns = pl.ds(pl.multiple_of(which * half, half), half)
        return jnp.dot(
            cross, cov[:, columns], precision=HIGHEST, preferred_element_type=jnp.float32
        )

    mix_out[...] = mixed_part(other)
    mix_copy = pltpu.make_async_remote_copy(
        src_ref=mix_out, dst_ref=mix_in, send_sem=mix_send, recv_sem=mix_recv,
        device_id=(me, other), device_id_type=MESH,
    )
    mix_copy.start()
    mixed_own = mixed_part(lab)

    def reduce_own():
        pltpu.make_async_copy(gpart.at[me], ggot.at[me], g_recv).start()
        pltpu.make_async_copy(ggot, ggot, g_recv).wait()
        gown[...] = jnp.sum(ggot[...].astype(jnp.float32), axis=0).astype(jnp.bfloat16)
        pltpu.make_async_copy(gown, gall.at[me], f_recv).start()

        def fan(k, c):
            send_fin(lax.rem(me + k, n))
            return c

        lax.fori_loop(1, n, fan, 0)

    if n == chunks:
        reduce_own()
    else:
        pl.when(me < chunks)(reduce_own)

    mix_copy.wait()
    mixed_ref[...] = (mixed_own + mix_in[...]).astype(jnp.bfloat16)

    pltpu.make_async_copy(gall, gall, f_recv).wait()
    for h in range(2):
        grad_ref[:, h * half:(h + 1) * half] = (
            gall[h * strips:(h + 1) * strips].reshape(half, half).astype(jnp.float32)
        )

    rest = slab_all.at[0, pl.ds(0, chips - 1)]
    pltpu.make_async_copy(rest, rest, slab_send).wait()
    rest = part.at[pl.ds(0, chips - 1)]
    pltpu.make_async_copy(rest, rest, part_send).wait()
    pltpu.make_async_copy(slab_all.at[0], slab_all.at[0], fwd_send).wait()
    pltpu.make_async_copy(pair_out, pair_out, pair_send).wait()

    def drain_grad(count):
        piece = gpart.at[pl.ds(0, count)]
        pltpu.make_async_copy(piece, piece, g_send).wait()

    def drain_fin():
        sent = ggot.at[pl.ds(0, n - 1)]
        pltpu.make_async_copy(sent, sent, f_send).wait()

    if n == chunks:
        drain_grad(chunks - 1)
        drain_fin()
    else:
        @pl.when(me < chunks)
        def _():
            drain_grad(chunks - 1)
            drain_fin()

        @pl.when(me >= chunks)
        def _():
            drain_grad(chunks)


def local(n, slab_points, key_points, length_weights, adjoint, label_cov, cotangent):
    rows, width = slab_points.shape
    keys, half = adjoint.shape
    labels = label_cov.shape[1]
    chunks = (half // CHUNK) * (labels // half)
    bf16, f32 = jnp.bfloat16, jnp.float32
    dma = pltpu.SemaphoreType.DMA
    chips = n // 2
    groups = chips // PAIR
    operands = (
        slab_points, key_points, length_weights.reshape(1, width), adjoint, label_cov, cotangent
    )
    return pl.pallas_call(
        functools.partial(kernel, n, chunks),
        out_shape=(
            pltpu.VMEM((rows, half), bf16),
            pltpu.VMEM((half, labels), f32),
        ),
        in_specs=[pl.BlockSpec(memory_space=pltpu.HBM)] * 6,
        out_specs=[pl.BlockSpec(memory_space=pltpu.VMEM)] * 2,
        scratch_shapes=[
            pltpu.VMEM((keys, width), bf16),
            pltpu.VMEM((1, width), f32),
            pltpu.VMEM((keys, half), bf16),
            pltpu.VMEM((half, labels), f32),
            pltpu.VMEM((2, rows, half), bf16),
            pltpu.VMEM((2, chips, rows, width), bf16),
            pltpu.VMEM((groups, PAIR * rows, half), f32),
            pltpu.VMEM((groups, PAIR * rows, half), f32),
            pltpu.VMEM((groups, PAIR * rows, half), f32),
            pltpu.VMEM((chips, rows, half), bf16),
            pltpu.VMEM((chips, rows, half), bf16),
            pltpu.VMEM((rows, half), f32),
            pltpu.VMEM((rows, half), f32),
            pltpu.VMEM((chunks, CHUNK, half), bf16),
            pltpu.VMEM((n, CHUNK, half), bf16),
            pltpu.VMEM((CHUNK, half), bf16),
            pltpu.VMEM((chunks, CHUNK, half), bf16),
            pltpu.VMEM((width, keys), bf16),
            pltpu.VMEM((1, keys), f32),
            dma((5,)),
            dma, dma((groups,)), dma, dma((groups,)), dma, dma((groups,)), dma, dma, dma, dma, dma, dma, dma, dma, dma, dma,
        ],
        compiler_params=pltpu.CompilerParams(
            collective_id=0, has_side_effects=True, vmem_limit_bytes=40 * 1024 * 1024
        ),
    )(*(pltpu.with_memory_space_constraint(x, pltpu.HBM) for x in operands))


def solution(mesh):
    placed = (P("pts", None), P("pts", None), P(), P("pts", "lab"), P("lab", None), P("pts", "lab"))
    return jax.shard_map(
        functools.partial(local, mesh.shape["pts"]),
        mesh=mesh,
        in_specs=placed,
        out_specs=(P("pts", "lab"), P("lab", None)),
        check_vma=False,
    )
```

```python
import functools

import jax
import jax.numpy as jnp
from jax import lax
from jax.experimental import pallas as pl
from jax.experimental.pallas import tpu as pltpu
from jax.sharding import PartitionSpec as P

MESH = pl.DeviceIdType.MESH
HIGHEST = lax.Precision.HIGHEST
PAIR = 2
CHUNK = 16


def kernel(
    n, chunks,
    slab_hbm, key_hbm, w_hbm, adj_hbm, cov_hbm, cot_hbm,
    mixed_ref, grad_ref,
    key, w, adj, cov, cot, slab_all, pair_out, pair_in, kept, part, got, mix_out, mix_in, gpart, ggot, gall,
    scaled_t, key_term,
    loc, slab_loc, slab_send, slab_recv, fwd_send, fwd_recv, pair_send, pair_recv, part_send, part_recv, cot_send, cot_recv,
    mix_send, mix_recv, g_send, g_recv, f_send, f_recv,
):
    me = lax.axis_index("pts")
    lab = lax.axis_index("lab")
    other = 1 - lab
    chip = me // 2
    core = lax.rem(me, 2)
    sibling = chip * 2 + 1 - core
    chips = n // 2
    groups = chips // PAIR
    g_me = chip // PAIR
    rows, width = slab_hbm.shape
    half = adj_hbm.shape[1]
    strips = half // CHUNK

    def greet(k, c):
        pl.semaphore_signal(
            barrier, inc=1, device_id=(lax.rem(me + k, n), lab), device_id_type=MESH
        )
        return c

    mine = slab_all.at[core, chip]
    slab_load = pltpu.make_async_copy(slab_hbm, mine, slab_loc)
    slab_load.start()
    barrier = pltpu.get_barrier_semaphore()
    lax.fori_loop(1, n, greet, 0)
    pl.semaphore_signal(barrier, inc=1, device_id=(me, other), device_id_type=MESH)

    loads = [
        pltpu.make_async_copy(src, dst, loc.at[i])
        for i, (src, dst) in enumerate(
            ((key_hbm, key), (w_hbm, w), (adj_hbm, adj), (cov_hbm, cov), (cot_hbm, cot.at[lab]))
        )
    ]
    for copy in loads:
        copy.start()
    slab_load.wait()
    pl.semaphore_wait(barrier, n)

    def send_slab(q):
        pltpu.make_async_remote_copy(
            src_ref=mine, dst_ref=mine, send_sem=slab_send,
            recv_sem=slab_recv.at[g_me], device_id=(q, lab), device_id_type=MESH,
        ).start()

    def member(g, j):
        return (g * PAIR + lax.rem(chip + j, PAIR)) * 2 + core

    def to_sibling(block, g):
        pltpu.make_async_remote_copy(
            src_ref=block, dst_ref=block, send_sem=fwd_send, recv_sem=fwd_recv.at[g],
            device_id=(sibling, lab), device_id_type=MESH,
        ).start()

    send_slab(member(g_me, 1))
    to_sibling(mine, g_me)

    def send_group(k, c):
        for j in range(PAIR):
            send_slab(member(lax.rem(g_me + groups - k, groups), j))
        return c

    lax.fori_loop(1, groups, send_group, 0)
    cot_copy = pltpu.make_async_remote_copy(
        src_ref=cot_hbm, dst_ref=cot.at[lab], send_sem=cot_send, recv_sem=cot_recv,
        device_id=(me, other), device_id_type=MESH,
    )
    cot_copy.start()

    loads[0].wait()
    loads[1].wait()
    w_row = w[...]
    w_col = jnp.broadcast_to(w_row, (8, width)).T[:, :1]
    key_t = key[...].astype(jnp.float32).T
    weighted = key_t * w_col
    scaled_t[...] = weighted.astype(jnp.bfloat16)
    key_term[...] = jnp.sum(weighted * key_t, axis=0, keepdims=True) * (-2.0 / width)

    def forward(g):
        block = slab_all.at[core, pl.ds(g * PAIR, PAIR)]
        pltpu.make_async_copy(block, block, slab_recv.at[g]).wait()
        to_sibling(block, g)

    def partial(g):
        block = slab_all.at[1 - core, pl.ds(g * PAIR, PAIR)]
        pltpu.make_async_copy(block, block, fwd_recv.at[g]).wait()
        own = slab_all[core, pl.ds(g * PAIR, PAIR)].reshape(PAIR * rows, width)
        s = jnp.concatenate([own, block[...].reshape(PAIR * rows, width)], axis=0)
        wide = s.astype(jnp.float32)
        s_term = jnp.sum(wide * wide * w_row, axis=1, keepdims=True) * (-2.0 / width)
        inner = jnp.dot(s, scaled_t[...], preferred_element_type=jnp.float32)
        tile = jnp.exp((s_term + key_term[...]) + inner * (4.0 / width)).astype(jnp.bfloat16)
        sums = jnp.dot(tile, adj[...], preferred_element_type=jnp.float32)
        pair_out[g] = sums[PAIR * rows:]
        pltpu.make_async_remote_copy(
            src_ref=pair_out.at[g], dst_ref=pair_in.at[g], send_sem=pair_send,
            recv_sem=pair_recv.at[g], device_id=(sibling, lab), device_id_type=MESH,
        ).start()
        kept[g] = sums[:PAIR * rows]

    def send_part(g, j):
        q = member(g, j)
        pltpu.make_async_remote_copy(
            src_ref=part.at[q // 2], dst_ref=got.at[chip], send_sem=part_send,
            recv_sem=part_recv, device_id=(q, lab), device_id_type=MESH,
        ).start()

    def collect(g):
        arrived = pair_in.at[g]
        pltpu.make_async_copy(arrived, arrived, pair_recv.at[g]).wait()
        both = (kept[g] + arrived[...]).astype(jnp.bfloat16)
        part[pl.ds(g * PAIR, PAIR)] = both.reshape(PAIR, rows, half)

    def group_at(k):
        return lax.rem(g_me + k, groups)

    near = slab_all.at[core, g_me * PAIR + lax.rem(chip + 1, PAIR)]
    pltpu.make_async_copy(near, near, slab_recv.at[g_me]).wait()
    to_sibling(near, g_me)
    loads[2].wait()

    def step(k, c):
        @pl.when(k + 1 < groups)
        def _():
            forward(group_at(k + 1))

        partial(group_at(k))

        @pl.when(k > 0)
        def _():
            g = group_at(k - 1)
            collect(g)

            @pl.when(k == 1)
            def _():
                pltpu.make_async_copy(part.at[chip], got.at[chip], part_recv).start()

            @pl.when(k > 1)
            def _():
                send_part(g, 0)

            send_part(g, 1)
        return c

    lax.fori_loop(0, groups, step, 0)
    g = group_at(groups - 1)
    collect(g)
    for j in range(PAIR):
        send_part(g, j)

    for copy in loads[3:]:
        copy.wait()
    cot_copy.wait()
    pltpu.make_async_copy(got, got, part_recv).wait()
    cross = jnp.sum(got[...].astype(jnp.float32), axis=0)

    cross_t = cross.T
    high = cross_t.astype(jnp.bfloat16)
    low = (cross_t - high.astype(jnp.float32)).astype(jnp.bfloat16)
    for h in range(2):
        c_half = cot[h]
        g_half = jnp.dot(high, c_half, preferred_element_type=jnp.float32) + jnp.dot(
            low, c_half, preferred_element_type=jnp.float32
        )
        gpart[h * strips:(h + 1) * strips] = g_half.astype(jnp.bfloat16).reshape(
            strips, CHUNK, half
        )

    def send_grad(q):
        pltpu.make_async_remote_copy(
            src_ref=gpart.at[q], dst_ref=ggot.at[me], send_sem=g_send,
            recv_sem=g_recv, device_id=(q, lab), device_id_type=MESH,
        ).start()

    def send_fin(q):
        pltpu.make_async_remote_copy(
            src_ref=gall.at[me], dst_ref=gall.at[me], send_sem=f_send,
            recv_sem=f_recv, device_id=(q, lab), device_id_type=MESH,
        ).start()

    def spread(k, c):
        send_grad(lax.rem(me + k, n))
        return c

    def spread_some(q, c):
        @pl.when(q != me)
        def _():
            send_grad(q)
        return c

    def keep_grad():
        pltpu.make_async_copy(gpart.at[me], ggot.at[me], g_recv).start()

    if n == chunks:
        lax.fori_loop(1, n, spread, 0)
        keep_grad()
    else:
        lax.fori_loop(0, chunks, spread_some, 0)
        pl.when(me < chunks)(keep_grad)

    def mixed_part(which):
        columns = pl.ds(pl.multiple_of(which * half, half), half)
        return jnp.dot(
            cross, cov[:, columns], precision=HIGHEST, preferred_element_type=jnp.float32
        )

    mix_out[...] = mixed_part(other)
    mix_copy = pltpu.make_async_remote_copy(
        src_ref=mix_out, dst_ref=mix_in, send_sem=mix_send, recv_sem=mix_recv,
        device_id=(me, other), device_id_type=MESH,
    )
    mix_copy.start()
    mixed_own = mixed_part(lab)

    def reduce_own():
        pltpu.make_async_copy(ggot, ggot, g_recv).wait()
        gall[me] = jnp.sum(ggot[...].astype(jnp.float32), axis=0).astype(jnp.bfloat16)

        def fan(k, c):
            send_fin(lax.rem(me + k, n))
            return c

        lax.fori_loop(1, n, fan, 0)

    if n == chunks:
        reduce_own()
    else:
        pl.when(me < chunks)(reduce_own)

    mix_copy.wait()
    mixed_ref[...] = (mixed_own + mix_in[...]).astype(jnp.bfloat16)

    def await_grad(count):
        pieces = gall.at[pl.ds(0, count)]
        pltpu.make_async_copy(pieces, pieces, f_recv).wait()

    if n == chunks:
        await_grad(chunks - 1)
    else:
        pl.when(me < chunks)(lambda: await_grad(chunks - 1))
        pl.when(me >= chunks)(lambda: await_grad(chunks))
    for h in range(2):
        grad_ref[:, h * half:(h + 1) * half] = (
            gall[h * strips:(h + 1) * strips].reshape(half, half).astype(jnp.float32)
        )

    rest = slab_all.at[0, pl.ds(0, chips - 1)]
    pltpu.make_async_copy(rest, rest, slab_send).wait()
    rest = part.at[pl.ds(0, chips - 1)]
    pltpu.make_async_copy(rest, rest, part_send).wait()
    pltpu.make_async_copy(slab_all.at[0], slab_all.at[0], fwd_send).wait()
    pltpu.make_async_copy(pair_out, pair_out, pair_send).wait()

    def drain_grad(count):
        piece = gpart.at[pl.ds(0, count)]
        pltpu.make_async_copy(piece, piece, g_send).wait()

    def drain_fin():
        sent = ggot.at[pl.ds(0, n - 1)]
        pltpu.make_async_copy(sent, sent, f_send).wait()

    if n == chunks:
        drain_grad(chunks - 1)
        drain_fin()
    else:
        @pl.when(me < chunks)
        def _():
            drain_grad(chunks - 1)
            drain_fin()

        @pl.when(me >= chunks)
        def _():
            drain_grad(chunks)


def local(n, slab_points, key_points, length_weights, adjoint, label_cov, cotangent):
    rows, width = slab_points.shape
    keys, half = adjoint.shape
    labels = label_cov.shape[1]
    chunks = (half // CHUNK) * (labels // half)
    bf16, f32 = jnp.bfloat16, jnp.float32
    dma = pltpu.SemaphoreType.DMA
    chips = n // 2
    groups = chips // PAIR
    operands = (
        slab_points, key_points, length_weights.reshape(1, width), adjoint, label_cov, cotangent
    )
    return pl.pallas_call(
        functools.partial(kernel, n, chunks),
        out_shape=(
            pltpu.VMEM((rows, half), bf16),
            pltpu.VMEM((half, labels), f32),
        ),
        in_specs=[pl.BlockSpec(memory_space=pltpu.HBM)] * 6,
        out_specs=[pl.BlockSpec(memory_space=pltpu.VMEM)] * 2,
        scratch_shapes=[
            pltpu.VMEM((keys, width), bf16),
            pltpu.VMEM((1, width), f32),
            pltpu.VMEM((keys, half), bf16),
            pltpu.VMEM((half, labels), f32),
            pltpu.VMEM((2, rows, half), bf16),
            pltpu.VMEM((2, chips, rows, width), bf16),
            pltpu.VMEM((groups, PAIR * rows, half), f32),
            pltpu.VMEM((groups, PAIR * rows, half), f32),
            pltpu.VMEM((groups, PAIR * rows, half), f32),
            pltpu.VMEM((chips, rows, half), bf16),
            pltpu.VMEM((chips, rows, half), bf16),
            pltpu.VMEM((rows, half), f32),
            pltpu.VMEM((rows, half), f32),
            pltpu.VMEM((chunks, CHUNK, half), bf16),
            pltpu.VMEM((n, CHUNK, half), bf16),
            pltpu.VMEM((chunks, CHUNK, half), bf16),
            pltpu.VMEM((width, keys), bf16),
            pltpu.VMEM((1, keys), f32),
            dma((5,)), dma,
            dma, dma((groups,)), dma, dma((groups,)), dma, dma((groups,)), dma, dma, dma, dma, dma, dma, dma, dma, dma, dma,
        ],
        compiler_params=pltpu.CompilerParams(
            collective_id=0, has_side_effects=True, vmem_limit_bytes=40 * 1024 * 1024
        ),
    )(*(pltpu.with_memory_space_constraint(x, pltpu.HBM) for x in operands))


def solution(mesh):
    placed = (P("pts", None), P("pts", None), P(), P("pts", "lab"), P("lab", None), P("pts", "lab"))
    return jax.shard_map(
        functools.partial(local, mesh.shape["pts"]),
        mesh=mesh,
        in_specs=placed,
        out_specs=(P("pts", "lab"), P("lab", None)),
        check_vma=False,
    )
```

```python
import functools

import jax
import jax.numpy as jnp
from jax import lax
from jax.experimental import pallas as pl
from jax.experimental.pallas import tpu as pltpu
from jax.sharding import PartitionSpec as P

MESH = pl.DeviceIdType.MESH
HIGHEST = lax.Precision.HIGHEST
PAIR = 2
CHUNK = 16


def kernel(
    n, chunks,
    slab_hbm, key_hbm, w_hbm, adj_hbm, cov_hbm, cot_hbm,
    mixed_ref, grad_ref,
    key, w, adj, cov, cot, slab_all, pair_out, pair_in, kept, part, got, mix_out, mix_in, gpart, ggot, gall,
    scaled_t, key_term,
    loc, slab_loc, slab_send, slab_recv, fwd_send, fwd_recv, pair_send, pair_recv, part_send, part_recv,
    cot_send, cot_recv, cot_pair_send, cot_pair_recv,
    mix_send, mix_recv, g_send, g_recv, f_send, f_recv,
):
    me = lax.axis_index("pts")
    lab = lax.axis_index("lab")
    other = 1 - lab
    chip = me // 2
    core = lax.rem(me, 2)
    sibling = chip * 2 + 1 - core
    chips = n // 2
    groups = chips // PAIR
    g_me = chip // PAIR
    rows, width = slab_hbm.shape
    half = adj_hbm.shape[1]
    strips = half // CHUNK

    def greet(k, c):
        pl.semaphore_signal(
            barrier, inc=1, device_id=(lax.rem(me + k, n), lab), device_id_type=MESH
        )
        return c

    mine = slab_all.at[core, chip]
    slab_load = pltpu.make_async_copy(slab_hbm, mine, slab_loc)
    slab_load.start()
    barrier = pltpu.get_barrier_semaphore()
    lax.fori_loop(1, n, greet, 0)
    pl.semaphore_signal(barrier, inc=1, device_id=(me, other), device_id_type=MESH)

    loads = [
        pltpu.make_async_copy(src, dst, loc.at[i])
        for i, (src, dst) in enumerate(
            ((key_hbm, key), (w_hbm, w), (adj_hbm, adj), (cov_hbm, cov), (cot_hbm, cot.at[lab, chip]))
        )
    ]
    for copy in loads:
        copy.start()
    slab_load.wait()
    pl.semaphore_wait(barrier, n)

    def send_slab(q):
        pltpu.make_async_remote_copy(
            src_ref=mine, dst_ref=mine, send_sem=slab_send,
            recv_sem=slab_recv.at[g_me], device_id=(q, lab), device_id_type=MESH,
        ).start()

    def member(g, j):
        return (g * PAIR + lax.rem(chip + j, PAIR)) * 2 + core

    def to_sibling(block, g):
        pltpu.make_async_remote_copy(
            src_ref=block, dst_ref=block, send_sem=fwd_send, recv_sem=fwd_recv.at[g],
            device_id=(sibling, lab), device_id_type=MESH,
        ).start()

    send_slab(member(g_me, 1))
    to_sibling(mine, g_me)

    def send_group(k, c):
        for j in range(PAIR):
            send_slab(member(lax.rem(g_me + groups - k, groups), j))
        return c

    lax.fori_loop(1, groups, send_group, 0)

    def send_cot(q):
        own = cot.at[lab, chip]
        pltpu.make_async_remote_copy(
            src_ref=own, dst_ref=own, send_sem=cot_send, recv_sem=cot_recv,
            device_id=(q, lab), device_id_type=MESH,
        ).start()

    def send_cots(k, c):
        for j in range(PAIR):
            send_cot(member(lax.rem(g_me + groups - k, groups), j))
        return c

    loads[4].wait()
    send_cot(member(g_me, 1))
    lax.fori_loop(1, groups, send_cots, 0)
    cot_copy = pltpu.make_async_remote_copy(
        src_ref=cot.at[lab], dst_ref=cot.at[lab], send_sem=cot_pair_send,
        recv_sem=cot_pair_recv, device_id=(me, other), device_id_type=MESH,
    )

    loads[0].wait()
    loads[1].wait()
    w_row = w[...]
    w_col = jnp.broadcast_to(w_row, (8, width)).T[:, :1]
    key_t = key[...].astype(jnp.float32).T
    weighted = key_t * w_col
    scaled_t[...] = weighted.astype(jnp.bfloat16)
    key_term[...] = jnp.sum(weighted * key_t, axis=0, keepdims=True) * (-2.0 / width)

    def forward(g):
        block = slab_all.at[core, pl.ds(g * PAIR, PAIR)]
        pltpu.make_async_copy(block, block, slab_recv.at[g]).wait()
        to_sibling(block, g)

    def partial(g):
        block = slab_all.at[1 - core, pl.ds(g * PAIR, PAIR)]
        pltpu.make_async_copy(block, block, fwd_recv.at[g]).wait()
        own = slab_all[core, pl.ds(g * PAIR, PAIR)].reshape(PAIR * rows, width)
        s = jnp.concatenate([own, block[...].reshape(PAIR * rows, width)], axis=0)
        wide = s.astype(jnp.float32)
        s_term = jnp.sum(wide * wide * w_row, axis=1, keepdims=True) * (-2.0 / width)
        inner = jnp.dot(s, scaled_t[...], preferred_element_type=jnp.float32)
        tile = jnp.exp((s_term + key_term[...]) + inner * (4.0 / width)).astype(jnp.bfloat16)
        sums = jnp.dot(tile, adj[...], preferred_element_type=jnp.float32)
        pair_out[g] = sums[PAIR * rows:]
        pltpu.make_async_remote_copy(
            src_ref=pair_out.at[g], dst_ref=pair_in.at[g], send_sem=pair_send,
            recv_sem=pair_recv.at[g], device_id=(sibling, lab), device_id_type=MESH,
        ).start()
        kept[g] = sums[:PAIR * rows]

    def send_part(g, j):
        q = member(g, j)
        pltpu.make_async_remote_copy(
            src_ref=part.at[q // 2], dst_ref=got.at[chip], send_sem=part_send,
            recv_sem=part_recv, device_id=(q, lab), device_id_type=MESH,
        ).start()

    def collect(g):
        arrived = pair_in.at[g]
        pltpu.make_async_copy(arrived, arrived, pair_recv.at[g]).wait()
        both = (kept[g] + arrived[...]).astype(jnp.bfloat16)
        part[pl.ds(g * PAIR, PAIR)] = both.reshape(PAIR, rows, half)

    def group_at(k):
        return lax.rem(g_me + k, groups)

    near = slab_all.at[core, g_me * PAIR + lax.rem(chip + 1, PAIR)]
    pltpu.make_async_copy(near, near, slab_recv.at[g_me]).wait()
    to_sibling(near, g_me)
    loads[2].wait()

    def step(k, c):
        @pl.when(k + 1 < groups)
        def _():
            forward(group_at(k + 1))

        partial(group_at(k))

        @pl.when(k > 0)
        def _():
            g = group_at(k - 1)
            collect(g)

            @pl.when(k == 1)
            def _():
                pltpu.make_async_copy(part.at[chip], got.at[chip], part_recv).start()
                arrived = cot.at[lab, pl.ds(0, chips - 1)]
                pltpu.make_async_copy(arrived, arrived, cot_recv).wait()
                cot_copy.start()

            @pl.when(k > 1)
            def _():
                send_part(g, 0)

            send_part(g, 1)
        return c

    lax.fori_loop(0, groups, step, 0)
    g = group_at(groups - 1)
    collect(g)
    for j in range(PAIR):
        send_part(g, j)

    cot_copy.wait()
    sums_t = part[...].reshape(chips * rows, half).astype(jnp.float32).T.astype(jnp.bfloat16)
    for h in range(2):
        g_half = jnp.dot(
            sums_t, cot[h].reshape(chips * rows, half), preferred_element_type=jnp.float32
        )
        gpart[h * strips:(h + 1) * strips] = g_half.astype(jnp.bfloat16).reshape(
            strips, CHUNK, half
        )

    def send_grad(q):
        pltpu.make_async_remote_copy(
            src_ref=gpart.at[q], dst_ref=ggot.at[me], send_sem=g_send,
            recv_sem=g_recv, device_id=(q, lab), device_id_type=MESH,
        ).start()

    def send_fin(q):
        pltpu.make_async_remote_copy(
            src_ref=gall.at[me], dst_ref=gall.at[me], send_sem=f_send,
            recv_sem=f_recv, device_id=(q, lab), device_id_type=MESH,
        ).start()

    def spread(k, c):
        send_grad(lax.rem(me + k, n))
        return c

    def spread_some(q, c):
        @pl.when(q != me)
        def _():
            send_grad(q)
        return c

    def keep_grad():
        pltpu.make_async_copy(gpart.at[me], ggot.at[me], g_recv).start()

    if n == chunks:
        lax.fori_loop(1, n, spread, 0)
        keep_grad()
    else:
        lax.fori_loop(0, chunks, spread_some, 0)
        pl.when(me < chunks)(keep_grad)

    loads[3].wait()
    pltpu.make_async_copy(got, got, part_recv).wait()
    cross = jnp.sum(got[...].astype(jnp.float32), axis=0)

    def mixed_part(which):
        columns = pl.ds(pl.multiple_of(which * half, half), half)
        return jnp.dot(
            cross, cov[:, columns], precision=HIGHEST, preferred_element_type=jnp.float32
        )

    mix_out[...] = mixed_part(other)
    mix_copy = pltpu.make_async_remote_copy(
        src_ref=mix_out, dst_ref=mix_in, send_sem=mix_send, recv_sem=mix_recv,
        device_id=(me, other), device_id_type=MESH,
    )
    mix_copy.start()

    def reduce_own():
        pltpu.make_async_copy(ggot, ggot, g_recv).wait()
        gall[me] = jnp.sum(ggot[...].astype(jnp.float32), axis=0).astype(jnp.bfloat16)

        def fan(k, c):
            send_fin(lax.rem(me + k, n))
            return c

        lax.fori_loop(1, n, fan, 0)

    if n == chunks:
        reduce_own()
    else:
        pl.when(me < chunks)(reduce_own)

    mixed_own = mixed_part(lab)
    mix_copy.wait()
    mixed_ref[...] = (mixed_own + mix_in[...]).astype(jnp.bfloat16)

    def await_grad(count):
        pieces = gall.at[pl.ds(0, count)]
        pltpu.make_async_copy(pieces, pieces, f_recv).wait()

    if n == chunks:
        await_grad(chunks - 1)
    else:
        pl.when(me < chunks)(lambda: await_grad(chunks - 1))
        pl.when(me >= chunks)(lambda: await_grad(chunks))
    for h in range(2):
        grad_ref[:, h * half:(h + 1) * half] = (
            gall[h * strips:(h + 1) * strips].reshape(half, half).astype(jnp.float32)
        )

    rest = slab_all.at[0, pl.ds(0, chips - 1)]
    pltpu.make_async_copy(rest, rest, slab_send).wait()
    rest = part.at[pl.ds(0, chips - 1)]
    pltpu.make_async_copy(rest, rest, part_send).wait()
    pltpu.make_async_copy(rest, rest, cot_send).wait()
    pltpu.make_async_copy(slab_all.at[0], slab_all.at[0], fwd_send).wait()
    pltpu.make_async_copy(pair_out, pair_out, pair_send).wait()

    def drain_grad(count):
        piece = gpart.at[pl.ds(0, count)]
        pltpu.make_async_copy(piece, piece, g_send).wait()

    def drain_fin():
        sent = ggot.at[pl.ds(0, n - 1)]
        pltpu.make_async_copy(sent, sent, f_send).wait()

    if n == chunks:
        drain_grad(chunks - 1)
        drain_fin()
    else:
        @pl.when(me < chunks)
        def _():
            drain_grad(chunks - 1)
            drain_fin()

        @pl.when(me >= chunks)
        def _():
            drain_grad(chunks)


def local(n, slab_points, key_points, length_weights, adjoint, label_cov, cotangent):
    rows, width = slab_points.shape
    keys, half = adjoint.shape
    labels = label_cov.shape[1]
    chunks = (half // CHUNK) * (labels // half)
    bf16, f32 = jnp.bfloat16, jnp.float32
    dma = pltpu.SemaphoreType.DMA
    chips = n // 2
    groups = chips // PAIR
    operands = (
        slab_points, key_points, length_weights.reshape(1, width), adjoint, label_cov, cotangent
    )
    return pl.pallas_call(
        functools.partial(kernel, n, chunks),
        out_shape=(
            pltpu.VMEM((rows, half), bf16),
            pltpu.VMEM((half, labels), f32),
        ),
        in_specs=[pl.BlockSpec(memory_space=pltpu.HBM)] * 6,
        out_specs=[pl.BlockSpec(memory_space=pltpu.VMEM)] * 2,
        scratch_shapes=[
            pltpu.VMEM((keys, width), bf16),
            pltpu.VMEM((1, width), f32),
            pltpu.VMEM((keys, half), bf16),
            pltpu.VMEM((half, labels), f32),
            pltpu.VMEM((2, chips, rows, half), bf16),
            pltpu.VMEM((2, chips, rows, width), bf16),
            pltpu.VMEM((groups, PAIR * rows, half), f32),
            pltpu.VMEM((groups, PAIR * rows, half), f32),
            pltpu.VMEM((groups, PAIR * rows, half), f32),
            pltpu.VMEM((chips, rows, half), bf16),
            pltpu.VMEM((chips, rows, half), bf16),
            pltpu.VMEM((rows, half), f32),
            pltpu.VMEM((rows, half), f32),
            pltpu.VMEM((chunks, CHUNK, half), bf16),
            pltpu.VMEM((n, CHUNK, half), bf16),
            pltpu.VMEM((chunks, CHUNK, half), bf16),
            pltpu.VMEM((width, keys), bf16),
            pltpu.VMEM((1, keys), f32),
            dma((5,)), dma,
            dma, dma((groups,)), dma, dma((groups,)), dma, dma((groups,)),
            *([dma] * 12),
        ],
        compiler_params=pltpu.CompilerParams(
            collective_id=0, has_side_effects=True, vmem_limit_bytes=40 * 1024 * 1024
        ),
    )(*(pltpu.with_memory_space_constraint(x, pltpu.HBM) for x in operands))


def solution(mesh):
    placed = (P("pts", None), P("pts", None), P(), P("pts", "lab"), P("lab", None), P("pts", "lab"))
    return jax.shard_map(
        functools.partial(local, mesh.shape["pts"]),
        mesh=mesh,
        in_specs=placed,
        out_specs=(P("pts", "lab"), P("lab", None)),
        check_vma=False,
    )
```

```python
import functools

import jax
import jax.numpy as jnp
from jax import lax
from jax.experimental import pallas as pl
from jax.experimental.pallas import tpu as pltpu
from jax.sharding import PartitionSpec as P

MESH = pl.DeviceIdType.MESH
HIGHEST = lax.Precision.HIGHEST
PAIR = 2
CHUNK = 16


def kernel(
    n, chunks,
    slab_hbm, key_hbm, w_hbm, adj_hbm, cov_hbm, cot_hbm,
    mixed_ref, grad_ref,
    key, w, adj, cov, cot, slab_all, pair_out, pair_in, kept, part, got, mix_out, mix_in, gpart, ggot, gall,
    scaled_t, key_term,
    loc, slab_loc, slab_send, slab_recv, fwd_send, fwd_recv, pair_send, pair_recv, part_send, part_recv,
    cot_send, cot_recv, cot_pair_send, cot_pair_recv,
    mix_send, mix_recv, g_send, g_recv, f_send, f_recv,
):
    me = lax.axis_index("pts")
    lab = lax.axis_index("lab")
    other = 1 - lab
    chip = me // 2
    core = lax.rem(me, 2)
    sibling = chip * 2 + 1 - core
    chips = n // 2
    groups = chips // PAIR
    g_me = chip // PAIR
    rows, width = slab_hbm.shape
    half = adj_hbm.shape[1]
    strips = half // CHUNK

    def greet(k, c):
        pl.semaphore_signal(
            barrier, inc=1, device_id=(lax.rem(me + k, n), lab), device_id_type=MESH
        )
        return c

    mine = slab_all.at[core, chip]
    slab_load = pltpu.make_async_copy(slab_hbm, mine, slab_loc)
    slab_load.start()
    barrier = pltpu.get_barrier_semaphore()
    lax.fori_loop(1, n, greet, 0)
    pl.semaphore_signal(barrier, inc=1, device_id=(me, other), device_id_type=MESH)

    loads = [
        pltpu.make_async_copy(src, dst, loc.at[i])
        for i, (src, dst) in enumerate(
            ((key_hbm, key), (w_hbm, w), (adj_hbm, adj), (cov_hbm, cov), (cot_hbm, cot.at[lab, chip]))
        )
    ]
    for copy in loads:
        copy.start()
    slab_load.wait()
    pl.semaphore_wait(barrier, n)

    def send_slab(q):
        pltpu.make_async_remote_copy(
            src_ref=mine, dst_ref=mine, send_sem=slab_send,
            recv_sem=slab_recv.at[g_me], device_id=(q, lab), device_id_type=MESH,
        ).start()

    def member(g, j):
        return (g * PAIR + lax.rem(chip + j, PAIR)) * 2 + core

    def to_sibling(block, g):
        pltpu.make_async_remote_copy(
            src_ref=block, dst_ref=block, send_sem=fwd_send, recv_sem=fwd_recv.at[g],
            device_id=(sibling, lab), device_id_type=MESH,
        ).start()

    send_slab(member(g_me, 1))
    to_sibling(mine, g_me)

    def send_group(k, c):
        for j in range(PAIR):
            send_slab(member(lax.rem(g_me + groups - k, groups), j))
        return c

    lax.fori_loop(1, groups, send_group, 0)

    def send_cot(q):
        own = cot.at[lab, chip]
        pltpu.make_async_remote_copy(
            src_ref=own, dst_ref=own, send_sem=cot_send, recv_sem=cot_recv.at[g_me],
            device_id=(q, lab), device_id_type=MESH,
        ).start()

    def send_cots(k, c):
        for j in range(PAIR):
            send_cot(member(lax.rem(g_me + groups - k, groups), j))
        return c

    loads[4].wait()
    send_cot(member(g_me, 1))
    lax.fori_loop(1, groups, send_cots, 0)

    def cot_over(block):
        pltpu.make_async_remote_copy(
            src_ref=block, dst_ref=block, send_sem=cot_pair_send,
            recv_sem=cot_pair_recv, device_id=(me, other), device_id_type=MESH,
        ).start()

    cot_over(cot.at[lab, chip])

    loads[0].wait()
    loads[1].wait()
    w_row = w[...]
    w_col = jnp.broadcast_to(w_row, (8, width)).T[:, :1]
    key_t = key[...].astype(jnp.float32).T
    weighted = key_t * w_col
    scaled_t[...] = weighted.astype(jnp.bfloat16)
    key_term[...] = jnp.sum(weighted * key_t, axis=0, keepdims=True) * (-2.0 / width)

    def forward(g):
        block = slab_all.at[core, pl.ds(g * PAIR, PAIR)]
        pltpu.make_async_copy(block, block, slab_recv.at[g]).wait()
        to_sibling(block, g)

    def partial(g):
        block = slab_all.at[1 - core, pl.ds(g * PAIR, PAIR)]
        pltpu.make_async_copy(block, block, fwd_recv.at[g]).wait()
        own = slab_all[core, pl.ds(g * PAIR, PAIR)].reshape(PAIR * rows, width)
        s = jnp.concatenate([own, block[...].reshape(PAIR * rows, width)], axis=0)
        wide = s.astype(jnp.float32)
        s_term = jnp.sum(wide * wide * w_row, axis=1, keepdims=True) * (-2.0 / width)
        inner = jnp.dot(s, scaled_t[...], preferred_element_type=jnp.float32)
        tile = jnp.exp((s_term + key_term[...]) + inner * (4.0 / width)).astype(jnp.bfloat16)
        sums = jnp.dot(tile, adj[...], preferred_element_type=jnp.float32)
        pair_out[g] = sums[PAIR * rows:]
        pltpu.make_async_remote_copy(
            src_ref=pair_out.at[g], dst_ref=pair_in.at[g], send_sem=pair_send,
            recv_sem=pair_recv.at[g], device_id=(sibling, lab), device_id_type=MESH,
        ).start()
        kept[g] = sums[:PAIR * rows]

    def send_part(g, j):
        q = member(g, j)
        pltpu.make_async_remote_copy(
            src_ref=part.at[q // 2], dst_ref=got.at[chip], send_sem=part_send,
            recv_sem=part_recv, device_id=(q, lab), device_id_type=MESH,
        ).start()

    def collect(g):
        arrived = pair_in.at[g]
        pltpu.make_async_copy(arrived, arrived, pair_recv.at[g]).wait()
        both = (kept[g] + arrived[...]).astype(jnp.bfloat16)
        part[pl.ds(g * PAIR, PAIR)] = both.reshape(PAIR, rows, half)

    def group_at(k):
        return lax.rem(g_me + k, groups)

    near = slab_all.at[core, g_me * PAIR + lax.rem(chip + 1, PAIR)]
    pltpu.make_async_copy(near, near, slab_recv.at[g_me]).wait()
    to_sibling(near, g_me)
    loads[2].wait()

    def step(k, c):
        @pl.when(k + 1 < groups)
        def _():
            forward(group_at(k + 1))

        partial(group_at(k))

        @pl.when(k == 0)
        def _():
            block = cot.at[lab, g_me * PAIR + lax.rem(chip + 1, PAIR)]
            pltpu.make_async_copy(block, block, cot_recv.at[g_me]).wait()
            cot_over(block)

        @pl.when(k > 0)
        def _():
            block = cot.at[lab, pl.ds(group_at(k) * PAIR, PAIR)]
            pltpu.make_async_copy(block, block, cot_recv.at[group_at(k)]).wait()
            cot_over(block)
            g = group_at(k - 1)
            collect(g)

            @pl.when(k == 1)
            def _():
                pltpu.make_async_copy(part.at[chip], got.at[chip], part_recv).start()

            @pl.when(k > 1)
            def _():
                send_part(g, 0)

            send_part(g, 1)
        return c

    lax.fori_loop(0, groups, step, 0)
    g = group_at(groups - 1)
    collect(g)
    for j in range(PAIR):
        send_part(g, j)

    pltpu.make_async_copy(cot.at[other], cot.at[other], cot_pair_recv).wait()
    sums_t = part[...].reshape(chips * rows, half).astype(jnp.float32).T.astype(jnp.bfloat16)
    for h in range(2):
        g_half = jnp.dot(
            sums_t, cot[h].reshape(chips * rows, half), preferred_element_type=jnp.float32
        )
        gpart[h * strips:(h + 1) * strips] = g_half.astype(jnp.bfloat16).reshape(
            strips, CHUNK, half
        )

    def send_grad(q):
        pltpu.make_async_remote_copy(
            src_ref=gpart.at[q], dst_ref=ggot.at[me], send_sem=g_send,
            recv_sem=g_recv, device_id=(q, lab), device_id_type=MESH,
        ).start()

    def send_fin(q):
        pltpu.make_async_remote_copy(
            src_ref=gall.at[me], dst_ref=gall.at[me], send_sem=f_send,
            recv_sem=f_recv, device_id=(q, lab), device_id_type=MESH,
        ).start()

    def spread(k, c):
        send_grad(lax.rem(me + k, n))
        return c

    def spread_some(q, c):
        @pl.when(q != me)
        def _():
            send_grad(q)
        return c

    def keep_grad():
        pltpu.make_async_copy(gpart.at[me], ggot.at[me], g_recv).start()

    if n == chunks:
        lax.fori_loop(1, n, spread, 0)
        keep_grad()
    else:
        lax.fori_loop(0, chunks, spread_some, 0)
        pl.when(me < chunks)(keep_grad)

    def reduce_own():
        pltpu.make_async_copy(ggot, ggot, g_recv).wait()
        gall[me] = jnp.sum(ggot[...].astype(jnp.float32), axis=0).astype(jnp.bfloat16)

        def fan(k, c):
            send_fin(lax.rem(me + k, n))
            return c

        lax.fori_loop(1, n, fan, 0)

    if n == chunks:
        reduce_own()
    else:
        pl.when(me < chunks)(reduce_own)

    loads[3].wait()
    pltpu.make_async_copy(got, got, part_recv).wait()
    cross = jnp.sum(got[...].astype(jnp.float32), axis=0)

    def mixed_part(which):
        columns = pl.ds(pl.multiple_of(which * half, half), half)
        return jnp.dot(
            cross, cov[:, columns], precision=HIGHEST, preferred_element_type=jnp.float32
        )

    mix_out[...] = mixed_part(other)
    mix_copy = pltpu.make_async_remote_copy(
        src_ref=mix_out, dst_ref=mix_in, send_sem=mix_send, recv_sem=mix_recv,
        device_id=(me, other), device_id_type=MESH,
    )
    mix_copy.start()

    mixed_own = mixed_part(lab)
    mix_copy.wait()
    mixed_ref[...] = (mixed_own + mix_in[...]).astype(jnp.bfloat16)

    def await_grad(count):
        pieces = gall.at[pl.ds(0, count)]
        pltpu.make_async_copy(pieces, pieces, f_recv).wait()

    if n == chunks:
        await_grad(chunks - 1)
    else:
        pl.when(me < chunks)(lambda: await_grad(chunks - 1))
        pl.when(me >= chunks)(lambda: await_grad(chunks))
    for h in range(2):
        grad_ref[:, h * half:(h + 1) * half] = (
            gall[h * strips:(h + 1) * strips].reshape(half, half).astype(jnp.float32)
        )

    rest = slab_all.at[0, pl.ds(0, chips - 1)]
    pltpu.make_async_copy(rest, rest, slab_send).wait()
    rest = part.at[pl.ds(0, chips - 1)]
    pltpu.make_async_copy(rest, rest, part_send).wait()
    pltpu.make_async_copy(rest, rest, cot_send).wait()
    pltpu.make_async_copy(cot.at[lab], cot.at[lab], cot_pair_send).wait()
    pltpu.make_async_copy(slab_all.at[0], slab_all.at[0], fwd_send).wait()
    pltpu.make_async_copy(pair_out, pair_out, pair_send).wait()

    def drain_grad(count):
        piece = gpart.at[pl.ds(0, count)]
        pltpu.make_async_copy(piece, piece, g_send).wait()

    def drain_fin():
        sent = ggot.at[pl.ds(0, n - 1)]
        pltpu.make_async_copy(sent, sent, f_send).wait()

    if n == chunks:
        drain_grad(chunks - 1)
        drain_fin()
    else:
        @pl.when(me < chunks)
        def _():
            drain_grad(chunks - 1)
            drain_fin()

        @pl.when(me >= chunks)
        def _():
            drain_grad(chunks)


def local(n, slab_points, key_points, length_weights, adjoint, label_cov, cotangent):
    rows, width = slab_points.shape
    keys, half = adjoint.shape
    labels = label_cov.shape[1]
    chunks = (half // CHUNK) * (labels // half)
    bf16, f32 = jnp.bfloat16, jnp.float32
    dma = pltpu.SemaphoreType.DMA
    chips = n // 2
    groups = chips // PAIR
    operands = (
        slab_points, key_points, length_weights.reshape(1, width), adjoint, label_cov, cotangent
    )
    return pl.pallas_call(
        functools.partial(kernel, n, chunks),
        out_shape=(
            pltpu.VMEM((rows, half), bf16),
            pltpu.VMEM((half, labels), f32),
        ),
        in_specs=[pl.BlockSpec(memory_space=pltpu.HBM)] * 6,
        out_specs=[pl.BlockSpec(memory_space=pltpu.VMEM)] * 2,
        scratch_shapes=[
            pltpu.VMEM((keys, width), bf16),
            pltpu.VMEM((1, width), f32),
            pltpu.VMEM((keys, half), bf16),
            pltpu.VMEM((half, labels), f32),
            pltpu.VMEM((2, chips, rows, half), bf16),
            pltpu.VMEM((2, chips, rows, width), bf16),
            pltpu.VMEM((groups, PAIR * rows, half), f32),
            pltpu.VMEM((groups, PAIR * rows, half), f32),
            pltpu.VMEM((groups, PAIR * rows, half), f32),
            pltpu.VMEM((chips, rows, half), bf16),
            pltpu.VMEM((chips, rows, half), bf16),
            pltpu.VMEM((rows, half), f32),
            pltpu.VMEM((rows, half), f32),
            pltpu.VMEM((chunks, CHUNK, half), bf16),
            pltpu.VMEM((n, CHUNK, half), bf16),
            pltpu.VMEM((chunks, CHUNK, half), bf16),
            pltpu.VMEM((width, keys), bf16),
            pltpu.VMEM((1, keys), f32),
            dma((5,)), dma,
            dma, dma((groups,)), dma, dma((groups,)), dma, dma((groups,)),
            *([dma] * 3), dma((groups,)), *([dma] * 8),
        ],
        compiler_params=pltpu.CompilerParams(
            collective_id=0, has_side_effects=True, vmem_limit_bytes=40 * 1024 * 1024
        ),
    )(*(pltpu.with_memory_space_constraint(x, pltpu.HBM) for x in operands))


def solution(mesh):
    placed = (P("pts", None), P("pts", None), P(), P("pts", "lab"), P("lab", None), P("pts", "lab"))
    return jax.shard_map(
        functools.partial(local, mesh.shape["pts"]),
        mesh=mesh,
        in_specs=placed,
        out_specs=(P("pts", "lab"), P("lab", None)),
        check_vma=False,
    )
```

```python
import functools

import jax
import jax.numpy as jnp
from jax import lax
from jax.experimental import pallas as pl
from jax.experimental.pallas import tpu as pltpu
from jax.sharding import PartitionSpec as P

MESH = pl.DeviceIdType.MESH
HIGHEST = lax.Precision.HIGHEST
PAIR = 2
CHUNK = 16


def kernel(
    n, chunks,
    slab_hbm, key_hbm, w_hbm, adj_hbm, cov_hbm, cot_hbm,
    mixed_ref, grad_ref,
    key, w, adj, cov, cot, slab_all, pair_out, pair_in, kept, part, got, mix_out, mix_in, gpart, ggot, gall,
    scaled_t, key_term,
    loc, slab_loc, slab_send, slab_recv, fwd_send, fwd_recv, pair_send, pair_recv, part_send, part_recv,
    cot_send, cot_recv, cot_pair_send, cot_pair_recv,
    mix_send, mix_recv, g_send, g_recv, f_send, f_recv,
):
    me = lax.axis_index("pts")
    lab = lax.axis_index("lab")
    other = 1 - lab
    chip = me // 2
    core = lax.rem(me, 2)
    sibling = chip * 2 + 1 - core
    chips = n // 2
    groups = chips // PAIR
    g_me = chip // PAIR
    rows, width = slab_hbm.shape
    half = adj_hbm.shape[1]
    strips = half // CHUNK

    def greet(k, c):
        pl.semaphore_signal(
            barrier, inc=1, device_id=(lax.rem(me + k, n), lab), device_id_type=MESH
        )
        return c

    mine = slab_all.at[core, chip]
    slab_load = pltpu.make_async_copy(slab_hbm, mine, slab_loc)
    slab_load.start()
    barrier = pltpu.get_barrier_semaphore()
    lax.fori_loop(1, n, greet, 0)
    pl.semaphore_signal(barrier, inc=1, device_id=(me, other), device_id_type=MESH)

    loads = [
        pltpu.make_async_copy(src, dst, loc.at[i])
        for i, (src, dst) in enumerate(
            ((key_hbm, key), (w_hbm, w), (adj_hbm, adj), (cov_hbm, cov), (cot_hbm, cot.at[lab, chip]))
        )
    ]
    for copy in loads:
        copy.start()
    slab_load.wait()
    pl.semaphore_wait(barrier, n)

    def send_slab(q):
        pltpu.make_async_remote_copy(
            src_ref=mine, dst_ref=mine, send_sem=slab_send,
            recv_sem=slab_recv.at[g_me], device_id=(q, lab), device_id_type=MESH,
        ).start()

    def member(g, j):
        return (g * PAIR + lax.rem(chip + j, PAIR)) * 2 + core

    def to_sibling(block, g):
        pltpu.make_async_remote_copy(
            src_ref=block, dst_ref=block, send_sem=fwd_send, recv_sem=fwd_recv.at[g],
            device_id=(sibling, lab), device_id_type=MESH,
        ).start()

    send_slab(member(g_me, 1))
    to_sibling(mine, g_me)

    def send_group(k, c):
        for j in range(PAIR):
            send_slab(member(lax.rem(g_me + groups - k, groups), j))
        return c

    lax.fori_loop(1, groups, send_group, 0)

    def send_cot(q):
        own = cot.at[lab, chip]
        pltpu.make_async_remote_copy(
            src_ref=own, dst_ref=own, send_sem=cot_send, recv_sem=cot_recv.at[g_me],
            device_id=(q, lab), device_id_type=MESH,
        ).start()

    def send_cots(k, c):
        for j in range(PAIR):
            send_cot(member(lax.rem(g_me + groups - k, groups), j))
        return c

    loads[4].wait()
    send_cot(member(g_me, 1))
    lax.fori_loop(1, groups, send_cots, 0)

    def cot_over(block):
        pltpu.make_async_remote_copy(
            src_ref=block, dst_ref=block, send_sem=cot_pair_send,
            recv_sem=cot_pair_recv, device_id=(me, other), device_id_type=MESH,
        ).start()

    cot_over(cot.at[lab, chip])

    loads[0].wait()
    loads[1].wait()
    w_row = w[...]
    w_col = jnp.broadcast_to(w_row, (8, width)).T[:, :1]
    key_t = key[...].astype(jnp.float32).T
    weighted = key_t * w_col
    scaled_t[...] = weighted.astype(jnp.bfloat16)
    key_term[...] = jnp.sum(weighted * key_t, axis=0, keepdims=True) * (-2.0 / width)

    def forward(g):
        block = slab_all.at[core, pl.ds(g * PAIR, PAIR)]
        pltpu.make_async_copy(block, block, slab_recv.at[g]).wait()
        to_sibling(block, g)

    def partial(g):
        block = slab_all.at[1 - core, pl.ds(g * PAIR, PAIR)]
        pltpu.make_async_copy(block, block, fwd_recv.at[g]).wait()
        own = slab_all[core, pl.ds(g * PAIR, PAIR)].reshape(PAIR * rows, width)
        s = jnp.concatenate([own, block[...].reshape(PAIR * rows, width)], axis=0)
        wide = s.astype(jnp.float32)
        s_term = jnp.sum(wide * wide * w_row, axis=1, keepdims=True) * (-2.0 / width)
        inner = jnp.dot(s, scaled_t[...], preferred_element_type=jnp.float32)
        tile = jnp.exp((s_term + key_term[...]) + inner * (4.0 / width)).astype(jnp.bfloat16)
        sums = jnp.dot(tile, adj[...], preferred_element_type=jnp.float32)
        pair_out[g] = sums[PAIR * rows:]
        pltpu.make_async_remote_copy(
            src_ref=pair_out.at[g], dst_ref=pair_in.at[g], send_sem=pair_send,
            recv_sem=pair_recv.at[g], device_id=(sibling, lab), device_id_type=MESH,
        ).start()
        kept[g] = sums[:PAIR * rows]

    def send_part(g, j):
        q = member(g, j)
        pltpu.make_async_remote_copy(
            src_ref=part.at[q // 2], dst_ref=got.at[chip], send_sem=part_send,
            recv_sem=part_recv, device_id=(q, lab), device_id_type=MESH,
        ).start()

    def collect(g):
        arrived = pair_in.at[g]
        pltpu.make_async_copy(arrived, arrived, pair_recv.at[g]).wait()
        both = (kept[g] + arrived[...]).astype(jnp.bfloat16)
        part[pl.ds(g * PAIR, PAIR)] = both.reshape(PAIR, rows, half)

    def group_at(k):
        return lax.rem(g_me + k, groups)

    near = slab_all.at[core, g_me * PAIR + lax.rem(chip + 1, PAIR)]
    pltpu.make_async_copy(near, near, slab_recv.at[g_me]).wait()
    to_sibling(near, g_me)
    forward(group_at(1))
    loads[2].wait()

    def step(k, c):
        @pl.when(k + 2 < groups)
        def _():
            forward(group_at(k + 2))

        partial(group_at(k))

        @pl.when(k == 0)
        def _():
            block = cot.at[lab, g_me * PAIR + lax.rem(chip + 1, PAIR)]
            pltpu.make_async_copy(block, block, cot_recv.at[g_me]).wait()
            cot_over(block)

        @pl.when(k > 0)
        def _():
            block = cot.at[lab, pl.ds(group_at(k) * PAIR, PAIR)]
            pltpu.make_async_copy(block, block, cot_recv.at[group_at(k)]).wait()
            cot_over(block)
            g = group_at(k - 1)
            collect(g)

            @pl.when(k == 1)
            def _():
                pltpu.make_async_copy(part.at[chip], got.at[chip], part_recv).start()

            @pl.when(k > 1)
            def _():
                send_part(g, 0)

            send_part(g, 1)
        return c

    lax.fori_loop(0, groups, step, 0)
    g = group_at(groups - 1)
    collect(g)
    for j in range(PAIR):
        send_part(g, j)

    pltpu.make_async_copy(cot.at[other], cot.at[other], cot_pair_recv).wait()
    sums_t = part[...].reshape(chips * rows, half).astype(jnp.float32).T.astype(jnp.bfloat16)
    for h in range(2):
        g_half = jnp.dot(
            sums_t, cot[h].reshape(chips * rows, half), preferred_element_type=jnp.float32
        )
        gpart[h * strips:(h + 1) * strips] = g_half.astype(jnp.bfloat16).reshape(
            strips, CHUNK, half
        )

    def send_grad(q):
        pltpu.make_async_remote_copy(
            src_ref=gpart.at[q], dst_ref=ggot.at[me], send_sem=g_send,
            recv_sem=g_recv, device_id=(q, lab), device_id_type=MESH,
        ).start()

    def send_fin(q):
        pltpu.make_async_remote_copy(
            src_ref=gall.at[me], dst_ref=gall.at[me], send_sem=f_send,
            recv_sem=f_recv, device_id=(q, lab), device_id_type=MESH,
        ).start()

    def spread(k, c):
        send_grad(lax.rem(me + k, n))
        return c

    def spread_some(q, c):
        @pl.when(q != me)
        def _():
            send_grad(q)
        return c

    def keep_grad():
        pltpu.make_async_copy(gpart.at[me], ggot.at[me], g_recv).start()

    if n == chunks:
        lax.fori_loop(1, n, spread, 0)
        keep_grad()
    else:
        lax.fori_loop(0, chunks, spread_some, 0)
        pl.when(me < chunks)(keep_grad)

    def reduce_own():
        pltpu.make_async_copy(ggot, ggot, g_recv).wait()
        gall[me] = jnp.sum(ggot[...].astype(jnp.float32), axis=0).astype(jnp.bfloat16)

        def fan(k, c):
            send_fin(lax.rem(me + k, n))
            return c

        lax.fori_loop(1, n, fan, 0)

    if n == chunks:
        reduce_own()
    else:
        pl.when(me < chunks)(reduce_own)

    loads[3].wait()
    pltpu.make_async_copy(got, got, part_recv).wait()
    cross = jnp.sum(got[...].astype(jnp.float32), axis=0)

    def mixed_part(which):
        columns = pl.ds(pl.multiple_of(which * half, half), half)
        return jnp.dot(
            cross, cov[:, columns], precision=HIGHEST, preferred_element_type=jnp.float32
        )

    mix_out[...] = mixed_part(other)
    mix_copy = pltpu.make_async_remote_copy(
        src_ref=mix_out, dst_ref=mix_in, send_sem=mix_send, recv_sem=mix_recv,
        device_id=(me, other), device_id_type=MESH,
    )
    mix_copy.start()

    mixed_own = mixed_part(lab)
    mix_copy.wait()
    mixed_ref[...] = (mixed_own + mix_in[...]).astype(jnp.bfloat16)

    def await_grad(count):
        pieces = gall.at[pl.ds(0, count)]
        pltpu.make_async_copy(pieces, pieces, f_recv).wait()

    if n == chunks:
        await_grad(chunks - 1)
    else:
        pl.when(me < chunks)(lambda: await_grad(chunks - 1))
        pl.when(me >= chunks)(lambda: await_grad(chunks))
    for h in range(2):
        grad_ref[:, h * half:(h + 1) * half] = (
            gall[h * strips:(h + 1) * strips].reshape(half, half).astype(jnp.float32)
        )

    rest = slab_all.at[0, pl.ds(0, chips - 1)]
    pltpu.make_async_copy(rest, rest, slab_send).wait()
    rest = part.at[pl.ds(0, chips - 1)]
    pltpu.make_async_copy(rest, rest, part_send).wait()
    pltpu.make_async_copy(rest, rest, cot_send).wait()
    pltpu.make_async_copy(cot.at[lab], cot.at[lab], cot_pair_send).wait()
    pltpu.make_async_copy(slab_all.at[0], slab_all.at[0], fwd_send).wait()
    pltpu.make_async_copy(pair_out, pair_out, pair_send).wait()

    def drain_grad(count):
        piece = gpart.at[pl.ds(0, count)]
        pltpu.make_async_copy(piece, piece, g_send).wait()

    def drain_fin():
        sent = ggot.at[pl.ds(0, n - 1)]
        pltpu.make_async_copy(sent, sent, f_send).wait()

    if n == chunks:
        drain_grad(chunks - 1)
        drain_fin()
    else:
        @pl.when(me < chunks)
        def _():
            drain_grad(chunks - 1)
            drain_fin()

        @pl.when(me >= chunks)
        def _():
            drain_grad(chunks)


def local(n, slab_points, key_points, length_weights, adjoint, label_cov, cotangent):
    rows, width = slab_points.shape
    keys, half = adjoint.shape
    labels = label_cov.shape[1]
    chunks = (half // CHUNK) * (labels // half)
    bf16, f32 = jnp.bfloat16, jnp.float32
    dma = pltpu.SemaphoreType.DMA
    chips = n // 2
    groups = chips // PAIR
    operands = (
        slab_points, key_points, length_weights.reshape(1, width), adjoint, label_cov, cotangent
    )
    return pl.pallas_call(
        functools.partial(kernel, n, chunks),
        out_shape=(
            pltpu.VMEM((rows, half), bf16),
            pltpu.VMEM((half, labels), f32),
        ),
        in_specs=[pl.BlockSpec(memory_space=pltpu.HBM)] * 6,
        out_specs=[pl.BlockSpec(memory_space=pltpu.VMEM)] * 2,
        scratch_shapes=[
            pltpu.VMEM((keys, width), bf16),
            pltpu.VMEM((1, width), f32),
            pltpu.VMEM((keys, half), bf16),
            pltpu.VMEM((half, labels), f32),
            pltpu.VMEM((2, chips, rows, half), bf16),
            pltpu.VMEM((2, chips, rows, width), bf16),
            pltpu.VMEM((groups, PAIR * rows, half), f32),
            pltpu.VMEM((groups, PAIR * rows, half), f32),
            pltpu.VMEM((groups, PAIR * rows, half), f32),
            pltpu.VMEM((chips, rows, half), bf16),
            pltpu.VMEM((chips, rows, half), bf16),
            pltpu.VMEM((rows, half), f32),
            pltpu.VMEM((rows, half), f32),
            pltpu.VMEM((chunks, CHUNK, half), bf16),
            pltpu.VMEM((n, CHUNK, half), bf16),
            pltpu.VMEM((chunks, CHUNK, half), bf16),
            pltpu.VMEM((width, keys), bf16),
            pltpu.VMEM((1, keys), f32),
            dma((5,)), dma,
            dma, dma((groups,)), dma, dma((groups,)), dma, dma((groups,)),
            *([dma] * 3), dma((groups,)), *([dma] * 8),
        ],
        compiler_params=pltpu.CompilerParams(
            collective_id=0, has_side_effects=True, vmem_limit_bytes=40 * 1024 * 1024
        ),
    )(*(pltpu.with_memory_space_constraint(x, pltpu.HBM) for x in operands))


def solution(mesh):
    placed = (P("pts", None), P("pts", None), P(), P("pts", "lab"), P("lab", None), P("pts", "lab"))
    return jax.shard_map(
        functools.partial(local, mesh.shape["pts"]),
        mesh=mesh,
        in_specs=placed,
        out_specs=(P("pts", "lab"), P("lab", None)),
        check_vma=False,
    )
```
